32 devices in a mesh: section: 2 (over core), ctx: 4 (over z), tensor: 4 (over y, x).
Axes of the slice: x: 2, y: 2, z: 4, core: 2. Of those that a mesh axis runs over, the one named last changes fastest.
Arguments:
- inputs: bfloat16 [2, 4, 2, 512, 1536], P(None, 'ctx', None, 'tensor', 'section'), may hold values from -6 to 6
- cotangent: bfloat16 [2, 4, 2, 512, 1536], P(None, 'ctx', None, 'tensor', 'section'), may hold values from -6 to 6
- block_order: int32 [8], replicated, may hold values from 0 to 7, as said below
- attn_gain: float32 [2, 1536], P('section'), may hold values from 0.1 to 1.9
- w_query: bfloat16 [2, 1536, 1536], P('section', None, 'tensor'), may hold values from -0.15625 to 0.15625
- key_weight: bfloat16 [2, 1536, 768], P('section', None, 'tensor'), may hold values from -0.15625 to 0.15625
- value_weight: bfloat16 [2, 1536, 768], P('section', None, 'tensor'), may hold values from -0.15625 to 0.15625
- w_out: bfloat16 [2, 1536, 1536], P('section', 'tensor'), may hold values from -3 to 3
- mlp_gain: float32 [2, 1536], P('section'), may hold values from 0.1 to 1.9
- w_gate: bfloat16 [2, 1536, 4096], P('section', None, 'tensor'), may hold values from -0.15625 to 0.15625
- w_up: bfloat16 [2, 1536, 4096], P('section', None, 'tensor'), may hold values from -0.15625 to 0.15625
- w_down: bfloat16 [2, 4096, 1536], P('section', 'tensor'), may hold values from -0.09375 to 0.09375
Outputs:
- block_output: bfloat16 [2, 4, 2, 512, 1536], P(None, 'ctx', None, 'tensor', 'section')
- input_grad: float32 [2, 4, 2, 512, 1536], P(None, 'ctx', None, 'tensor', 'section')
- grad_attn_gain: float32 [2, 1536], P('section')
- grad_w_query: float32 [2, 1536, 1536], P('section', None, 'tensor')
- grad_w_key: float32 [2, 1536, 768], P('section', None, 'tensor')
- grad_w_value: float32 [2, 1536, 768], P('section', None, 'tensor')
- grad_w_out: float32 [2, 1536, 1536], P('section', 'tensor')
- grad_mlp_gain: float32 [2, 1536], P('section')
- grad_w_gate: float32 [2, 1536, 4096], P('section', None, 'tensor')
- grad_w_up: float32 [2, 1536, 4096], P('section', None, 'tensor')
- grad_w_down: float32 [2, 4096, 1536], P('section', 'tensor')
The draws below stay inside these ranges and needn't reach their ends.
Inputs may be any that keep to these rules, and one draw needn't show every extreme that they name: Mirrored pairs: block_order[2 c] and block_order[2 c + 1] are c and 7 - c, in either order, so context rank c stores one early and one late block of positions (each 512 long); every block occurs once.
All inputs are finite; a program needn't handle non-finite values.
Results may differ from the reference program's by a relative error of at most 0.039.
Values may be sent and summed in bfloat16 or wider, within the bound.
A program may use at most 512 MiB of HBM per device.

```python
import jax
import jax.numpy as jnp
from jax import lax

MODEL_DIM = 1536
QUERY_HEADS = 16
KV_HEAD_COUNT = 8
HEAD_DIM = 96
FF = 4096
SEQUENCE_TOKENS = 4096
SEQS = 2
RELAY_SECTIONS = 2
BLOCK_LEN = 512
N_CTX = 4


def draw_block_order(key, part):
    key = jax.random.fold_in(key, 11)
    flips = jax.random.randint(key, (N_CTX,), 0, 2).astype(jnp.int32)
    ranks = jnp.arange(N_CTX, dtype=jnp.int32)
    mirror = 2 * N_CTX - 1 - ranks
    first = jnp.where(flips == 1, mirror, ranks)
    second = jnp.where(flips == 1, ranks, mirror)
    return jnp.stack([first, second], axis=1).reshape(2 * N_CTX).astype(jnp.int32)


def levels(own_key, dims, split, smallest, high):
    def one(axis_at, shards_of):
        steps = jax.random.uniform(jax.random.fold_in(jax.random.fold_in(own_key, 6), axis_at), (shards_of,), jnp.float32, smallest / len(split), high / len(split))
        return jnp.repeat(jnp.exp(steps), dims[axis_at] // shards_of).reshape((-1,) + (1,) * (len(dims) - axis_at - 1))

    level = one(*split[0])
    for cut in split[1:]:
        level = level * one(*cut)
    return level


def normal_values(own_key, dims, spread, limit, shards=(), kind=jnp.bfloat16):
    result = jax.random.normal(own_key, dims, jnp.float32) * spread
    if len(shards) > 0:
        result = levels(own_key, dims, shards, -0.22, 0.18) * result
    return jnp.clip(result, min=-limit, max=limit).astype(kind)


def setup_inputs(seed: int = 0) -> dict:
    streams_of = jax.random.split(jax.random.key(seed), 13)
    return {
        "inputs": normal_values(streams_of[0], (SEQS, N_CTX, 2, BLOCK_LEN, MODEL_DIM), 1.0, 6.0, ((1, 4), (3, 4), (4, 2))),
        "cotangent": normal_values(streams_of[1], (SEQS, N_CTX, 2, BLOCK_LEN, MODEL_DIM), 1.0, 6.0, ((1, 4), (3, 4), (4, 2))),
        "block_order": draw_block_order(jax.random.fold_in(streams_of[12], 71), 0),
        "attn_gain": jnp.clip(1.0 + 0.18 * jax.random.normal(streams_of[3], (RELAY_SECTIONS, MODEL_DIM), jnp.float32), 0.1, 1.9),
        "w_query": normal_values(streams_of[4], (RELAY_SECTIONS, MODEL_DIM, QUERY_HEADS * HEAD_DIM), MODEL_DIM ** -0.5, 0.15625, ((0, 2), (2, 4))),
        "key_weight": normal_values(streams_of[5], (RELAY_SECTIONS, MODEL_DIM, KV_HEAD_COUNT * HEAD_DIM), MODEL_DIM ** -0.5, 0.15625, ((0, 2), (2, 4))),
        "value_weight": normal_values(streams_of[6], (RELAY_SECTIONS, MODEL_DIM, KV_HEAD_COUNT * HEAD_DIM), MODEL_DIM ** -0.5, 0.15625, ((0, 2), (2, 4))),
        "w_out": normal_values(streams_of[7], (RELAY_SECTIONS, QUERY_HEADS * HEAD_DIM, MODEL_DIM), 4 ** -0.5, 3.0, ((0, 2), (1, 4))),
        "mlp_gain": jnp.clip(1.0 + 0.18 * jax.random.normal(streams_of[8], (RELAY_SECTIONS, MODEL_DIM), jnp.float32), 0.1, 1.9),
        "w_gate": normal_values(streams_of[9], (RELAY_SECTIONS, MODEL_DIM, FF), MODEL_DIM ** -0.5, 0.15625, ((0, 2), (2, 4))),
        "w_up": normal_values(streams_of[10], (RELAY_SECTIONS, MODEL_DIM, FF), MODEL_DIM ** -0.5, 0.15625, ((0, 2), (2, 4))),
        "w_down": normal_values(streams_of[11], (RELAY_SECTIONS, FF, MODEL_DIM), FF ** -0.5, 0.09375, ((0, 2), (1, 4))),
    }


@jax.custom_vjp
def lower_precision(v):
    return lax.optimization_barrier(v.astype(jnp.bfloat16)).astype(jnp.float32)

@jax.custom_vjp
def lower_precision_back(v):
    return v

def low_keep(v):
    return (lower_precision(v), None)

def low_pass(kept, grad):
    return (grad,)

def back_keep(v):
    return (v, None)

def back_low(kept, grad):
    return (lower_precision(grad),)
lower_precision.defvjp(low_keep, low_pass)
lower_precision_back.defvjp(back_keep, back_low)
EPSILON = 1e-05
ROPE_BASE = 100000.0
PRECISE = lax.Precision.HIGHEST

def matrix_product(left, right):
    return jnp.dot(left, right, precision=PRECISE, preferred_element_type=jnp.float32)

def rms_norm(operand, gain_vec):
    return operand * lax.rsqrt(lax.optimization_barrier(jnp.mean(operand * operand, axis=-1, keepdims=True)) + EPSILON) * gain_vec

def rope_tables(positions):
    exponent = jnp.arange(0, HEAD_DIM, 2).astype(jnp.float32) / HEAD_DIM
    frequency = ROPE_BASE ** (-exponent)
    phases = positions.astype(jnp.float32)[:, None] * frequency[None, :]
    phases = jnp.concatenate([phases, phases], axis=-1)
    return (jnp.cos(phases), jnp.sin(phases))

def rotate(operand, cosine, sine):
    half_size = operand.shape[-1] // 2
    turned = jnp.concatenate([-operand[..., half_size:], operand[..., :half_size]], axis=-1)
    return operand * cosine[:, None, :] + turned * sine[:, None, :]

def attend_block(query_rows, query_pos, projected_keys, projected_values, key_pos):
    raw_scores = jnp.einsum('bhgd,khd->hgbk', query_rows, projected_keys, precision=PRECISE)
    scores = lower_precision_back(raw_scores) * HEAD_DIM ** (-0.5)
    visible = query_pos[:, None] >= key_pos[None, :]
    scores = jnp.where(visible[None, None], scores, -1e+30)
    largest = lax.optimization_barrier(jnp.max(scores, axis=-1, keepdims=True))
    powers = jnp.exp(scores - largest)
    attn_probs = lower_precision(powers / lax.optimization_barrier(jnp.sum(powers, axis=-1, keepdims=True)))
    return jnp.einsum('hgbk,khd->bhgd', attn_probs, projected_values, precision=PRECISE)

def layer(stream, params, cosine, sine, positions):
    attn_gain, w_query, key_weight, value_weight, w_out, mlp_gain, w_gate, w_up, w_down = params
    group_width = QUERY_HEADS // KV_HEAD_COUNT
    rows_per_block = min(512, SEQUENCE_TOKENS)
    normalized_input = lower_precision(rms_norm(stream, attn_gain))
    query_rows = matrix_product(normalized_input, w_query).reshape(SEQUENCE_TOKENS, QUERY_HEADS, HEAD_DIM)
    query_rows = lower_precision(rotate(lower_precision_back(query_rows), cosine, sine))
    projected_keys = matrix_product(normalized_input, key_weight).reshape(SEQUENCE_TOKENS, KV_HEAD_COUNT, HEAD_DIM)
    projected_keys = lower_precision(rotate(lower_precision_back(projected_keys), cosine, sine))
    projected_values = lower_precision(lower_precision_back(matrix_product(normalized_input, value_weight).reshape(SEQUENCE_TOKENS, KV_HEAD_COUNT, HEAD_DIM)))
    query_block_list = query_rows.reshape(SEQUENCE_TOKENS // rows_per_block, rows_per_block, KV_HEAD_COUNT, group_width, HEAD_DIM)
    pos_blocks = positions.reshape(SEQUENCE_TOKENS // rows_per_block, rows_per_block)
    checked = jax.checkpoint(attend_block)
    mixed_heads = lax.map(lambda operands: checked(operands[0], operands[1], projected_keys, projected_values, positions), (query_block_list, pos_blocks))
    mixed_heads = lower_precision(lower_precision_back(mixed_heads.reshape(SEQUENCE_TOKENS, QUERY_HEADS * HEAD_DIM)))
    middle = stream + lower_precision_back(matrix_product(mixed_heads, w_out))
    normed_two = lower_precision(rms_norm(middle, mlp_gain))
    gate_value = lower_precision_back(matrix_product(normed_two, w_gate))
    up_value = lower_precision_back(matrix_product(normed_two, w_up))
    activated = lower_precision(gate_value * jax.nn.sigmoid(gate_value) * up_value)
    return middle + lower_precision_back(matrix_product(activated, w_down))

def reference(inputs, cotangent, block_order, attn_gain, w_query, key_weight, value_weight, w_out, mlp_gain, w_gate, w_up, w_down):
    block_len = SEQUENCE_TOKENS // (2 * N_CTX)
    positions = (block_order.astype(jnp.int32)[:, None] * block_len + jnp.arange(block_len, dtype=jnp.int32)[None, :]).reshape(SEQUENCE_TOKENS)
    cosine, sine = rope_tables(positions)
    streams = inputs.astype(jnp.float32).reshape(SEQS, SEQUENCE_TOKENS, MODEL_DIM)
    weights = tuple((stacked.astype(jnp.float32) for stacked in (attn_gain, w_query, key_weight, value_weight, w_out, mlp_gain, w_gate, w_up, w_down)))

    def run(all_streams, all_weights):
        first_params = tuple((stacked[0] for stacked in all_weights))
        second_params = tuple((stacked[1] for stacked in all_weights))

        def one_sequence(carried, stream):
            handed = lower_precision(lower_precision_back(layer(stream, first_params, cosine, sine, positions)))
            return (carried, layer(handed, second_params, cosine, sine, positions))
        unused, outputs = lax.scan(one_sequence, jnp.zeros((), jnp.float32), all_streams)
        return outputs
    outputs, pullback = jax.vjp(run, streams, weights)
    grad_in, grads_all = pullback(cotangent.astype(jnp.float32).reshape(SEQS, SEQUENCE_TOKENS, MODEL_DIM))
    out_shape = (SEQS, N_CTX, 2, block_len, MODEL_DIM)
    return (outputs.reshape(out_shape).astype(jnp.bfloat16), grad_in.reshape(out_shape), grads_all[0], grads_all[1], grads_all[2], grads_all[3], grads_all[4], grads_all[5], grads_all[6], grads_all[7], grads_all[8])
```

```python
import jax
import jax.numpy as jnp
import numpy as np
from jax import lax
from jax.experimental import pallas as pl
from jax.experimental.pallas import tpu as pltpu
from jax.sharding import PartitionSpec as P

HEAD_DIM = 96
EPSILON = 1e-05
ROPE_BASE = 100000.0
LOG2E = 1.4426950408889634
BF = jnp.bfloat16
F32 = jnp.float32


def nn(a, b):
    return lax.dot_general(a, b, (((1,), (0,)), ((), ())), preferred_element_type=F32)


def nt(a, b):
    return lax.dot_general(a, b, (((1,), (1,)), ((), ())), preferred_element_type=F32)


def tn(a, b):
    return lax.dot_general(a, b, (((0,), (0,)), ((), ())), preferred_element_type=F32)


def head_of(x, h):
    return x[:, h * HEAD_DIM : (h + 1) * HEAD_DIM]


def transposed(x):
    return x.astype(F32).T.astype(BF)


def causal(length):
    keys = lax.broadcasted_iota(jnp.int32, (length, length), 0)
    queries = lax.broadcasted_iota(jnp.int32, (length, length), 1)
    return keys <= queries


def fwd_kernel(order_ref, own_ref, q_ref, kv_ref, mix_ref, mixt_ref, lse_ref, qt, m_s, l_s, acc):
    n_ctx, n_t, _, sp, width = kv_ref.shape
    length = n_t * sp
    kv_heads = width // (2 * HEAD_DIM)
    q_heads = q_ref.shape[-1] // HEAD_DIM
    group = q_heads // kv_heads
    scale = HEAD_DIM**-0.5 * LOG2E
    for j in range(2):
        x = q_ref[:, j].reshape(length, -1)
        for h in range(q_heads):
            qt[j, h] = transposed(head_of(x, h))
    m_s[...] = jnp.full_like(m_s, -1e30)
    l_s[...] = jnp.zeros_like(l_s)
    acc[...] = jnp.zeros_like(acc)

    def body(k, _):
        c_at = k // 2
        j_at = lax.rem(k, 2)
        key_block = order_ref[k]
        x = kv_ref[c_at, :, pl.ds(j_at, 1)].reshape(length, width)
        keys = [head_of(x, h) for h in range(kv_heads)]
        values = [transposed(head_of(x, kv_heads + h)) for h in range(kv_heads)]

        def step(j, masked):
            for h in range(q_heads):
                s = nn(keys[h // group], qt[j, h]) * scale
                if masked:
                    s = jnp.where(causal(length), s, -1e30)
                m_old = m_s[j, h]
                m_new = jnp.maximum(m_old, jnp.max(s, axis=0, keepdims=True))
                alpha = jnp.exp2(m_old - m_new)
                p = jnp.exp2(s - m_new)
                l_s[j, h] = l_s[j, h] * alpha + jnp.sum(p, axis=0, keepdims=True)
                m_s[j, h] = m_new
                acc[j, h] = acc[j, h] * alpha + nn(values[h // group], p.astype(BF))

        for j in range(2):
            own_block = own_ref[j]

            @pl.when(key_block < own_block)
            def _():
                step(j, False)

            @pl.when(key_block == own_block)
            def _():
                step(j, True)

        return 0

    lax.fori_loop(0, 2 * n_ctx, body, 0)
    for j in range(2):
        outs = []
        for h in range(q_heads):
            out = acc[j, h] / l_s[j, h]
            mixt_ref[j, h] = out.astype(BF)
            lse_ref[j, h] = m_s[j, h] + jnp.log2(l_s[j, h])
            outs.append(out.T)
        mix_ref[:, j] = jnp.concatenate(outs, axis=-1).astype(BF).reshape(n_t, sp, -1)


def flash_forward(order, own, q, kv):
    n_ctx, n_t, _, sp, width = kv.shape
    q_heads = q.shape[-1] // HEAD_DIM
    length = n_t * sp
    vm = pl.BlockSpec(memory_space=pltpu.VMEM)
    sm = pl.BlockSpec(memory_space=pltpu.SMEM)
    rows = (2, q_heads, 1, length)
    cols = (2, q_heads, HEAD_DIM, length)
    return pl.pallas_call(
        fwd_kernel,
        out_shape=(
            jax.ShapeDtypeStruct(q.shape, BF),
            jax.ShapeDtypeStruct(cols, BF),
            jax.ShapeDtypeStruct(rows, F32),
        ),
        in_specs=[sm, sm, vm, vm],
        out_specs=(vm, vm, vm),
        scratch_shapes=[
            pltpu.VMEM(cols, BF),
            pltpu.VMEM(rows, F32),
            pltpu.VMEM(rows, F32),
            pltpu.VMEM(cols, F32),
        ],
        compiler_params=pltpu.CompilerParams(vmem_limit_bytes=48 * 2**20),
    )(order, own, q, kv)


def bwd_kernel(
    order_ref, own_ref, q_ref, kv_ref, do_ref, mixt_ref, lse_ref, cos_ref, sin_ref,
    dq_ref, dkv_ref, qt, dot, qn, don, dl_s, dqt,
):
    n_ctx, n_t, _, sp, width = kv_ref.shape
    length = n_t * sp
    kv_heads = width // (2 * HEAD_DIM)
    q_heads = q_ref.shape[-1] // HEAD_DIM
    group = q_heads // kv_heads
    scale = HEAD_DIM**-0.5
    for j in range(2):
        x = q_ref[:, j].reshape(length, -1)
        y = do_ref[:, j].reshape(length, -1)
        for h in range(q_heads):
            a = head_of(x, h)
            qn[j, h] = a
            qt[j, h] = transposed(a)
            b = head_of(y, h)
            don[j, h] = b
            bt = b.astype(F32).T
            dot[j, h] = bt.astype(BF)
            dl_s[j, h] = jnp.sum(bt * mixt_ref[j, h].astype(F32), axis=0, keepdims=True)
    dqt[...] = jnp.zeros_like(dqt)

    def body(k, _):
        c_at = k // 2
        j_at = lax.rem(k, 2)
        key_block = order_ref[k]
        x = kv_ref[c_at, :, pl.ds(j_at, 1)].reshape(length, width)
        for kh in range(kv_heads):
            key = head_of(x, kh)
            value = head_of(x, kv_heads + kh)
            key_t = transposed(key)

            def step(j, masked, dk, dv):
                for g in range(group):
                    h = kh * group + g
                    s = nn(key, qt[j, h]) * (scale * LOG2E)
                    p = jnp.exp2(s - lse_ref[j, h])
                    if masked:
                        p = jnp.where(causal(length), p, 0.0)
                    dp = nn(value, dot[j, h])
                    ds = (p * (dp - dl_s[j, h])).astype(BF)
                    dv = dv + nn(p.astype(BF), don[j, h])
                    dk = dk + nn(ds, qn[j, h])
                    dqt[j, h] += nn(key_t, ds)
                return dk, dv

            dk = jnp.zeros((length, HEAD_DIM), F32)
            dv = dk
            for j in range(2):
                own_block = own_ref[j]
                dk, dv = lax.cond(
                    key_block < own_block,
                    lambda a, b: step(j, False, a, b),
                    lambda a, b: lax.cond(
                        key_block == own_block,
                        lambda a, b: step(j, True, a, b),
                        lambda a, b: (a, b),
                        a,
                        b,
                    ),
                    dk,
                    dv,
                )
            at = pl.ds(j_at, 1)
            shape = (n_t, 1, sp, HEAD_DIM)
            lo, hi = kh * HEAD_DIM, (kv_heads + kh) * HEAD_DIM
            dkv_ref[c_at, :, at, :, lo : lo + HEAD_DIM] = (dk * scale).astype(BF).reshape(shape)
            dkv_ref[c_at, :, at, :, hi : hi + HEAD_DIM] = dv.astype(BF).reshape(shape)
        return 0

    lax.fori_loop(0, 2 * n_ctx, body, 0)
    half = HEAD_DIM // 2
    for j in range(2):
        outs = []
        for h in range(q_heads):
            d = dqt[j, h] * scale
            sc = d * sin_ref[j]
            back = d * cos_ref[j] + jnp.concatenate([sc[half:], -sc[:half]], axis=0)
            outs.append(back.T)
        dq_ref[:, j] = jnp.concatenate(outs, axis=-1).astype(BF).reshape(n_t, sp, -1)


def flash_backward(order, own, q, kv, do, mixt, lse, cos_t, sin_t):
    n_ctx, n_t, _, sp, width = kv.shape
    q_heads = q.shape[-1] // HEAD_DIM
    length = n_t * sp
    vm = pl.BlockSpec(memory_space=pltpu.VMEM)
    sm = pl.BlockSpec(memory_space=pltpu.SMEM)
    cols = pltpu.VMEM((2, q_heads, HEAD_DIM, length), BF)
    natural = pltpu.VMEM((2, q_heads, length, HEAD_DIM), BF)
    return pl.pallas_call(
        bwd_kernel,
        out_shape=(jax.ShapeDtypeStruct(q.shape, BF), jax.ShapeDtypeStruct(kv.shape, BF)),
        in_specs=[sm, sm] + [vm] * 7,
        out_specs=(vm, vm),
        scratch_shapes=[
            cols,
            cols,
            natural,
            natural,
            pltpu.VMEM((2, q_heads, 1, length), F32),
            pltpu.VMEM((2, q_heads, HEAD_DIM, length), F32),
        ],
        compiler_params=pltpu.CompilerParams(vmem_limit_bytes=48 * 2**20),
    )(order, own, q, kv, do, mixt, lse, cos_t, sin_t)


def rms_norm(v, gain):
    return v * lax.rsqrt(jnp.mean(v * v, axis=-1, keepdims=True) + EPSILON) * gain


def silu_product(gate, up):
    return gate * jax.nn.sigmoid(gate) * up


def turn_matrix(heads, total):
    half = HEAD_DIM // 2
    m = np.zeros((total, total), np.float32)
    for h in range(heads):
        at = h * HEAD_DIM
        for i in range(half):
            m[at + half + i, at + i] = -1.0
            m[at + i, at + half + i] = 1.0
    return m


def swap(value):
    return lax.ppermute(value, "section", [(0, 1), (1, 0)])


def gather_rows(x):
    return lax.all_gather(x, "tensor", axis=0)


def scatter_rows(x):
    return lax.psum_scatter(x.astype(BF), "tensor", scatter_dimension=0).astype(F32)


def on_device(
    inputs, cotangent, block_order, attn_gain, w_query, key_weight, value_weight, w_out,
    mlp_gain, w_gate, w_up, w_down,
):
    sec = lax.axis_index("section")
    first = sec == 0
    ctx = lax.axis_index("ctx")
    n_t = lax.axis_size("tensor")
    n_ctx = lax.axis_size("ctx")
    _, _, _, sp, half_width = inputs.shape
    length = sp * n_t
    d = 2 * half_width
    rows = n_t * 2 * sp
    wq, wk, wv = w_query[0], key_weight[0], value_weight[0]
    q_w, kv_w = wq.shape[1], 2 * wk.shape[1]
    qkv_w = q_w + kv_w
    q_heads, kv_heads = q_w // HEAD_DIM, kv_w // (2 * HEAD_DIM)

    def to_own(x):
        keep = lax.dynamic_index_in_dim(x[:, 0], sec, 0, keepdims=False)
        give = lax.dynamic_index_in_dim(x[:, 0], 1 - sec, 0, keepdims=False)
        got = swap(give)
        return jnp.where(
            first, jnp.concatenate([keep, got], -1), jnp.concatenate([got, keep], -1)
        )

    def from_own(y, out_dtype):
        lo, hi = y[..., :half_width], y[..., half_width:]
        keep = jnp.where(first, lo, hi)
        got = swap(jnp.where(first, hi, lo).astype(BF)).astype(y.dtype)
        return jnp.where(first, jnp.stack([keep, got]), jnp.stack([got, keep]))[
            :, None
        ].astype(out_dtype)

    x_own = to_own(inputs)
    g_own = to_own(cotangent)

    turn_q = jnp.asarray(turn_matrix(q_heads, q_w), BF)
    turn_kv = turn_matrix(kv_heads, kv_w)
    wkv = jnp.concatenate([wk, wv], 1)
    wcat = jnp.concatenate(
        [wq, wkv, nn(wq, turn_q).astype(BF), nn(wkv, jnp.asarray(turn_kv, BF)).astype(BF)], 1
    )

    def both(w):
        return lax.all_gather(w, "section", axis=0)

    wcat2, wo2, wg2, wu2, wd2, gains2 = (
        both(wcat), both(w_out[0]), both(w_gate[0]), both(w_up[0]), both(w_down[0]),
        both(jnp.concatenate([attn_gain, mlp_gain], 0)),
    )

    own = lax.dynamic_slice_in_dim(block_order, 2 * ctx, 2, 0)
    offs = jnp.arange(length, dtype=jnp.int32)
    pos = own[:, None] * length + offs[None, :]
    freq = ROPE_BASE ** (-(jnp.arange(0, HEAD_DIM, 2).astype(F32) / HEAD_DIM))
    phase_t = freq[None, :, None] * pos.astype(F32)[:, None, :]
    phase_t = jnp.concatenate([phase_t, phase_t], 1)
    cos_t, sin_t = jnp.cos(phase_t), jnp.sin(phase_t)

    def rows_of(t):
        t = jnp.swapaxes(t, 1, 2).reshape(2, n_t, sp, HEAD_DIM)
        return jnp.swapaxes(t, 0, 1).reshape(rows, HEAD_DIM)

    cos_r, sin_r = rows_of(cos_t), rows_of(sin_t)
    ones = jnp.ones((rows, kv_w // 2), F32)
    cos_kv = jnp.concatenate([jnp.tile(cos_r, (1, kv_heads)), ones], 1)
    sin_kv = jnp.concatenate([jnp.tile(sin_r, (1, kv_heads)), 0 * ones], 1)
    cos_all = jnp.concatenate([jnp.tile(cos_r, (1, q_heads)), cos_kv], 1)
    sin_all = jnp.concatenate([jnp.tile(sin_r, (1, q_heads)), sin_kv], 1)

    def forward(h, layer):
        a_gain, m_gain = gains2[layer, 0], gains2[layer, 1]
        n1 = gather_rows(rms_norm(h, a_gain).astype(BF)).reshape(rows, d)
        raw = nn(n1, wcat2[layer])
        qkv = (raw[:, :qkv_w] * cos_all + raw[:, qkv_w:] * sin_all).astype(BF)
        q = qkv[:, :q_w].reshape(n_t, 2, sp, q_w)
        kv = lax.all_gather(qkv[:, q_w:].reshape(n_t, 2, sp, kv_w), "ctx", axis=0)
        mix, mixt, lse = flash_forward(block_order, own, q, kv)
        part = nn(mix.reshape(rows, q_w), wo2[layer])
        h2 = h + scatter_rows(part.reshape(n_t, 2, sp, d))
        n2 = gather_rows(rms_norm(h2, m_gain).astype(BF)).reshape(rows, d)
        gate, up = nn(n2, wg2[layer]), nn(n2, wu2[layer])
        act = silu_product(gate, up).astype(BF)
        out = h2 + scatter_rows(nn(act, wd2[layer]).reshape(n_t, 2, sp, d))
        return out, (h, n1, q, kv, mix, mixt, lse, h2, n2, gate, up, act)

    def reduce_grad(g):
        g = lax.psum_scatter(g.astype(BF), "section", scatter_dimension=0, tiled=True)
        return lax.psum(g, "ctx")

    def backward(g, gm, layer, kept):
        h, n1, q, kv, mix, mixt, lse, h2, n2, gate, up, act = kept
        a_gain, m_gain = gains2[layer, 0], gains2[layer, 1]
        gm = gather_rows(gm).reshape(rows, d)
        dact = nt(gm, wd2[layer])
        _, pull = jax.vjp(silu_product, gate, up)
        dgate, dup = pull(dact)
        dgate, dup = dgate.astype(BF), dup.astype(BF)
        dn2 = scatter_rows((nt(dgate, wg2[layer]) + nt(dup, wu2[layer])).reshape(n_t, 2, sp, d))
        _, pull = jax.vjp(rms_norm, h2, m_gain)
        dh2, d_mg = pull(dn2)
        dh2 = g + dh2
        ga = gather_rows(dh2.astype(BF)).reshape(rows, d)
        dmix = nt(ga, wo2[layer]).astype(BF)
        dq, dkv = flash_backward(
            block_order, own, q, kv, dmix.reshape(n_t, 2, sp, q_w), mixt, lse, cos_t, sin_t
        )
        dkv = lax.psum_scatter(dkv, "ctx", scatter_dimension=0).astype(F32).reshape(rows, kv_w)
        turned = lax.dot_general(
            dkv * sin_kv,
            jnp.asarray(-turn_kv),
            (((1,), (0,)), ((), ())),
            precision=lax.Precision.HIGHEST,
            preferred_element_type=F32,
        )
        dkv = (dkv * cos_kv + turned).astype(BF)
        dqkv = jnp.concatenate([dq.reshape(rows, q_w), dkv], 1)
        dn1 = scatter_rows(nt(dqkv, wcat2[layer][:, :qkv_w]).reshape(n_t, 2, sp, d))
        _, pull = jax.vjp(rms_norm, h, a_gain)
        dh, d_ag = pull(dn1)
        dh = dh2 + dh
        grads = (
            reduce_grad(tn(act, gm)),
            reduce_grad(tn(n2, dgate)),
            reduce_grad(tn(n2, dup)),
            reduce_grad(tn(mix.reshape(rows, q_w), ga)),
            reduce_grad(tn(n1, dqkv)),
        )
        return dh, (d_ag, d_mg), grads

    out0, kept0 = forward(x_own.astype(F32), 0)
    y, kept1 = forward(out0.astype(BF).astype(F32), 1)
    dh1, gains1, grads1 = backward(g_own.astype(F32), g_own, 1, kept1)
    g0 = dh1.astype(BF)
    dh0, gains0, grads0 = backward(g0.astype(F32), g0, 0, kept0)

    gain_sum = lax.psum(jnp.stack([jnp.stack(gains0), jnp.stack(gains1)]), ("section", "ctx", "tensor"))
    gain_own = lax.dynamic_index_in_dim(gain_sum, sec, 0, keepdims=False)

    def to_owner(r0, r1):
        got = swap(jnp.where(first, r1, r0))
        keep = jnp.where(first, r0, r1)
        return jnp.where(
            first, jnp.concatenate([keep, got], 0), jnp.concatenate([got, keep], 0)
        ).astype(F32)

    gd, gg, gu, go, gqkv = (to_owner(a, b) for a, b in zip(grads0, grads1))
    half_kv = kv_w // 2
    return (
        from_own(y, BF),
        from_own(dh0, F32),
        gain_own[0:1],
        gqkv[None, :, :q_w],
        gqkv[None, :, q_w : q_w + half_kv],
        gqkv[None, :, q_w + half_kv :],
        go[None],
        gain_own[1:2],
        gg[None],
        gu[None],
        gd[None],
    )


def solution(mesh):
    rows = P(None, "ctx", None, "tensor", "section")
    gain = P("section", None)
    col = P("section", None, "tensor")
    row = P("section", "tensor", None)
    return jax.shard_map(
        on_device,
        mesh=mesh,
        in_specs=(rows, rows, P(), gain, col, col, col, row, gain, col, col, row),
        out_specs=(rows, rows, gain, col, col, col, row, gain, col, col, row),
        check_vma=False,
    )
```

```python
import functools

import jax
import jax.numpy as jnp
import numpy as np
from jax import lax
from jax.experimental import pallas as pl
from jax.experimental.pallas import tpu as pltpu
from jax.sharding import PartitionSpec as P

HEAD_DIM = 96
EPSILON = 1e-05
ROPE_BASE = 100000.0
LOG2E = 1.4426950408889634
BF = jnp.bfloat16
F32 = jnp.float32


def nn(a, b):
    return lax.dot_general(a, b, (((1,), (0,)), ((), ())), preferred_element_type=F32)


def nt(a, b):
    return lax.dot_general(a, b, (((1,), (1,)), ((), ())), preferred_element_type=F32)


def tn(a, b):
    return lax.dot_general(a, b, (((0,), (0,)), ((), ())), preferred_element_type=F32)


def head_of(x, h):
    return x[:, h * HEAD_DIM : (h + 1) * HEAD_DIM]


def transposed(x):
    return x.astype(F32).T.astype(BF)


def causal(length):
    keys = lax.broadcasted_iota(jnp.int32, (length, length), 0)
    queries = lax.broadcasted_iota(jnp.int32, (length, length), 1)
    return keys <= queries


def fwd_kernel(order_ref, own_ref, q_ref, kv_ref, mix_ref, mixt_ref, lse_ref, qt, m_s, l_s, acc):
    n_ctx, n_t, _, sp, width = kv_ref.shape
    length = n_t * sp
    kv_heads = width // (2 * HEAD_DIM)
    q_heads = q_ref.shape[-1] // HEAD_DIM
    group = q_heads // kv_heads
    scale = HEAD_DIM**-0.5 * LOG2E
    for j in range(2):
        x = q_ref[:, j].reshape(length, -1)
        for h in range(q_heads):
            qt[j, h] = transposed(head_of(x, h))
    m_s[...] = jnp.full_like(m_s, -1e30)
    l_s[...] = jnp.zeros_like(l_s)
    acc[...] = jnp.zeros_like(acc)

    def body(k, _):
        c_at = k // 2
        j_at = lax.rem(k, 2)
        key_block = order_ref[k]
        x = kv_ref[c_at, :, pl.ds(j_at, 1)].reshape(length, width)
        keys = [head_of(x, h) for h in range(kv_heads)]
        values = [transposed(head_of(x, kv_heads + h)) for h in range(kv_heads)]

        def step(j, masked):
            for h in range(q_heads):
                s = nn(keys[h // group], qt[j, h]) * scale
                if masked:
                    s = jnp.where(causal(length), s, -1e30)
                m_old = m_s[j, h]
                m_new = jnp.maximum(m_old, jnp.max(s, axis=0, keepdims=True))
                alpha = jnp.exp2(m_old - m_new)
                p = jnp.exp2(s - m_new)
                l_s[j, h] = l_s[j, h] * alpha + jnp.sum(p, axis=0, keepdims=True)
                m_s[j, h] = m_new
                acc[j, h] = acc[j, h] * alpha + nn(values[h // group], p.astype(BF))

        for j in range(2):
            own_block = own_ref[j]

            @pl.when(key_block < own_block)
            def _():
                step(j, False)

            @pl.when(key_block == own_block)
            def _():
                step(j, True)

        return 0

    lax.fori_loop(0, 2 * n_ctx, body, 0)
    for j in range(2):
        outs = []
        for h in range(q_heads):
            out = acc[j, h] / l_s[j, h]
            mixt_ref[j, h] = out.astype(BF)
            lse_ref[j, h] = m_s[j, h] + jnp.log2(l_s[j, h])
            outs.append(out.T)
        mix_ref[:, j] = jnp.concatenate(outs, axis=-1).astype(BF).reshape(n_t, sp, -1)


def flash_forward(order, own, q, kv):
    n_ctx, n_t, _, sp, width = kv.shape
    q_heads = q.shape[-1] // HEAD_DIM
    length = n_t * sp
    vm = pl.BlockSpec(memory_space=pltpu.VMEM)
    sm = pl.BlockSpec(memory_space=pltpu.SMEM)
    rows = (2, q_heads, 1, length)
    cols = (2, q_heads, HEAD_DIM, length)
    return pl.pallas_call(
        fwd_kernel,
        out_shape=(
            jax.ShapeDtypeStruct(q.shape, BF),
            jax.ShapeDtypeStruct(cols, BF),
            jax.ShapeDtypeStruct(rows, F32),
        ),
        in_specs=[sm, sm, vm, vm],
        out_specs=(vm, vm, vm),
        scratch_shapes=[
            pltpu.VMEM(cols, BF),
            pltpu.VMEM(rows, F32),
            pltpu.VMEM(rows, F32),
            pltpu.VMEM(cols, F32),
        ],
        compiler_params=pltpu.CompilerParams(vmem_limit_bytes=48 * 2**20),
    )(order, own, q, kv)


def bwd_kernel(
    order_ref, own_ref, q_ref, kv_ref, do_ref, mixt_ref, lse_ref, cos_ref, sin_ref,
    dq_ref, dkv_ref, qt, dot, qn, don, dl_s, dqt,
):
    n_ctx, n_t, _, sp, width = kv_ref.shape
    length = n_t * sp
    kv_heads = width // (2 * HEAD_DIM)
    q_heads = q_ref.shape[-1] // HEAD_DIM
    group = q_heads // kv_heads
    scale = HEAD_DIM**-0.5
    for j in range(2):
        x = q_ref[:, j].reshape(length, -1)
        y = do_ref[:, j].reshape(length, -1)
        for h in range(q_heads):
            a = head_of(x, h)
            qn[j, h] = a
            qt[j, h] = transposed(a)
            b = head_of(y, h)
            don[j, h] = b
            bt = b.astype(F32).T
            dot[j, h] = bt.astype(BF)
            dl_s[j, h] = jnp.sum(bt * mixt_ref[j, h].astype(F32), axis=0, keepdims=True)
    dqt[...] = jnp.zeros_like(dqt)

    def body(k, _):
        c_at = k // 2
        j_at = lax.rem(k, 2)
        key_block = order_ref[k]
        x = kv_ref[c_at, :, pl.ds(j_at, 1)].reshape(length, width)
        for kh in range(kv_heads):
            key = head_of(x, kh)
            value = head_of(x, kv_heads + kh)
            key_t = transposed(key)

            def step(j, masked, dk, dv):
                for g in range(group):
                    h = kh * group + g
                    s = nn(key, qt[j, h]) * (scale * LOG2E)
                    p = jnp.exp2(s - lse_ref[j, h])
                    if masked:
                        p = jnp.where(causal(length), p, 0.0)
                    dp = nn(value, dot[j, h])
                    ds = (p * (dp - dl_s[j, h])).astype(BF)
                    dv = dv + nn(p.astype(BF), don[j, h])
                    dk = dk + nn(ds, qn[j, h])
                    dqt[j, h] += nn(key_t, ds)
                return dk, dv

            dk = jnp.zeros((length, HEAD_DIM), F32)
            dv = dk
            for j in range(2):
                own_block = own_ref[j]
                dk, dv = lax.cond(
                    key_block < own_block,
                    lambda a, b: step(j, False, a, b),
                    lambda a, b: lax.cond(
                        key_block == own_block,
                        lambda a, b: step(j, True, a, b),
                        lambda a, b: (a, b),
                        a,
                        b,
                    ),
                    dk,
                    dv,
                )
            at = pl.ds(j_at, 1)
            shape = (n_t, 1, sp, HEAD_DIM)
            lo, hi = kh * HEAD_DIM, (kv_heads + kh) * HEAD_DIM
            dkv_ref[c_at, :, at, :, lo : lo + HEAD_DIM] = (dk * scale).astype(BF).reshape(shape)
            dkv_ref[c_at, :, at, :, hi : hi + HEAD_DIM] = dv.astype(BF).reshape(shape)
        return 0

    lax.fori_loop(0, 2 * n_ctx, body, 0)
    half = HEAD_DIM // 2
    for j in range(2):
        outs = []
        for h in range(q_heads):
            d = dqt[j, h] * scale
            sc = d * sin_ref[j]
            back = d * cos_ref[j] + jnp.concatenate([sc[half:], -sc[:half]], axis=0)
            outs.append(back.T)
        dq_ref[:, j] = jnp.concatenate(outs, axis=-1).astype(BF).reshape(n_t, sp, -1)


def flash_backward(order, own, q, kv, do, mixt, lse, cos_t, sin_t):
    n_ctx, n_t, _, sp, width = kv.shape
    q_heads = q.shape[-1] // HEAD_DIM
    length = n_t * sp
    vm = pl.BlockSpec(memory_space=pltpu.VMEM)
    sm = pl.BlockSpec(memory_space=pltpu.SMEM)
    cols = pltpu.VMEM((2, q_heads, HEAD_DIM, length), BF)
    natural = pltpu.VMEM((2, q_heads, length, HEAD_DIM), BF)
    return pl.pallas_call(
        bwd_kernel,
        out_shape=(jax.ShapeDtypeStruct(q.shape, BF), jax.ShapeDtypeStruct(kv.shape, BF)),
        in_specs=[sm, sm] + [vm] * 7,
        out_specs=(vm, vm),
        scratch_shapes=[
            cols,
            cols,
            natural,
            natural,
            pltpu.VMEM((2, q_heads, 1, length), F32),
            pltpu.VMEM((2, q_heads, HEAD_DIM, length), F32),
        ],
        compiler_params=pltpu.CompilerParams(vmem_limit_bytes=48 * 2**20),
    )(order, own, q, kv, do, mixt, lse, cos_t, sin_t)


def silu_product(gate, up):
    return gate * jax.nn.sigmoid(gate) * up


MESH = pl.DeviceIdType.MESH


def tensor_peers():
    t = lax.axis_index("tensor")
    return t, t + 1 - 2 * lax.rem(t, 2), lax.rem(t + 2, 4), 3 - t


def greet(*peers):
    barrier = pltpu.get_barrier_semaphore()
    for peer in peers:
        pl.semaphore_signal(barrier, inc=1, device_id={"tensor": peer}, device_id_type=MESH)
    pl.semaphore_wait(barrier, len(peers))


def send(src, dst, sems, at, peer):
    return pltpu.make_async_remote_copy(
        src_ref=src,
        dst_ref=dst,
        send_sem=sems[0].at[at],
        recv_sem=sems[1].at[at],
        device_id={"tensor": peer},
        device_id_type=MESH,
    )


def gather_start(full, sems, chunks, q):
    t, x, y, _ = tensor_peers()
    j, at = chunks[q]
    near, far = (x, y) if j == 0 else (y, x)
    own = full.at[t, j, at]
    send(own, own, sems, (q, 0), near).start()
    send(own, own, sems, (q, 1), far).start()


def gather_pass(full, sems, chunks, q):
    _, x, y, _ = tensor_peers()
    j, at = chunks[q]
    near, far = (x, y) if j == 0 else (y, x)
    got = full.at[near, j, at]
    send(got, got, sems, (q, 0), near).wait_recv()
    send(got, got, sems, (q, 2), far).start()


def gather_end(full, sems, chunks, q):
    t, x, y, diag = tensor_peers()
    j, at = chunks[q]
    near, far = (x, y) if j == 0 else (y, x)
    for kind, owner in ((1, far), (2, diag)):
        got = full.at[owner, j, at]
        send(got, got, sems, (q, kind), far).wait_recv()


def gather_drain(full, sems, chunks, q):
    t, x, _, _ = tensor_peers()
    j, at = chunks[q]
    own = full.at[t, j, at]
    for kind in range(3):
        send(own, own, sems, (q, kind), x).wait_send()


def scatter_start(part, got, sems, chunks, q):
    _, x, y, diag = tensor_peers()
    j, at = chunks[q]
    far = y if j == 0 else x
    send(part.at[diag, j, at], got.at[0, j, at], sems, (q, 0), far).start()
    send(part.at[far, j, at], got.at[2, j, at], sems, (q, 2), far).start()


def scatter_pass(part, got, held, sems, chunks, q):
    _, x, y, _ = tensor_peers()
    j, at = chunks[q]
    near = x if j == 0 else y
    send(held.at[j, at], got.at[0, j, at], sems, (q, 0), near).wait_recv()
    held[j, at] = (part[near, j, at].astype(F32) + got[0, j, at].astype(F32)).astype(BF)
    send(held.at[j, at], got.at[1, j, at], sems, (q, 1), near).start()


def scatter_end(part, got, held, sems, chunks, q):
    t, x, _, _ = tensor_peers()
    j, at = chunks[q]
    for kind in (2, 1):
        send(held.at[j, at], got.at[kind, j, at], sems, (q, kind), x).wait_recv()
    return (
        part[t, j, at].astype(F32) + got[1, j, at].astype(F32) + got[2, j, at].astype(F32)
    )


def scatter_drain(part, got, sems, chunks, q):
    t, x, _, _ = tensor_peers()
    j, at = chunks[q]
    for kind in range(3):
        send(part.at[t, j, at], got.at[kind, j, at], sems, (q, kind), x).wait_send()


def inverse_rms(v):
    return lax.rsqrt(jnp.mean(v * v, axis=-1, keepdims=True) + EPSILON)


def norm_back(v, gain, dn):
    r = inverse_rms(v)
    unit = v * r
    scaled = dn * gain
    dv = r * (scaled - unit * jnp.mean(scaled * unit, axis=-1, keepdims=True))
    return dv, jnp.sum(dn * unit, axis=0, keepdims=True)


def chunk_list(sp):
    parts = 2
    size = sp // parts
    return [(j, pl.ds(s * size, size)) for s in range(parts) for j in range(2)]


def run_exchange(sp, part, finish, full, got, held, sc_sems, ga_sems):
    chunks = chunk_list(sp)
    n = range(len(chunks))
    _, x, y, _ = tensor_peers()
    greet(x, y)
    if part is not None:
        for q in n:
            scatter_start(part, got, sc_sems, chunks, q)
        for q in n:
            scatter_pass(part, got, held, sc_sems, chunks, q)
    for q in n:
        j, at = chunks[q]
        total = None if part is None else scatter_end(part, got, held, sc_sems, chunks, q)
        finish(j, at, total)
        if full is not None:
            gather_start(full, ga_sems, chunks, q)
    if full is not None:
        for q in n:
            gather_pass(full, ga_sems, chunks, q)
        for q in n:
            gather_end(full, ga_sems, chunks, q)
        for q in n:
            gather_drain(full, ga_sems, chunks, q)
    if part is not None:
        for q in n:
            scatter_drain(part, got, sc_sems, chunks, q)


def scatter_scratch(sp, d):
    n = len(chunk_list(sp))
    return [
        pltpu.VMEM((3, 2, sp, d), BF),
        pltpu.VMEM((2, sp, d), BF),
        pltpu.SemaphoreType.DMA((n, 3)),
        pltpu.SemaphoreType.DMA((n, 3)),
    ]


def gather_scratch(sp):
    n = len(chunk_list(sp))
    return [pltpu.SemaphoreType.DMA((n, 3)), pltpu.SemaphoreType.DMA((n, 3))]


def call(kernel, out_shape, scratch, ident, *operands):
    vm = pl.BlockSpec(memory_space=pltpu.VMEM)
    return pl.pallas_call(
        kernel,
        out_shape=out_shape,
        in_specs=[vm] * len(operands),
        out_specs=(vm,) * len(out_shape),
        scratch_shapes=scratch,
        compiler_params=pltpu.CompilerParams(
            collective_id=ident, has_side_effects=True, vmem_limit_bytes=50 * 2**20
        ),
    )(*operands)


def shapes_of(h):
    _, sp, d = h.shape
    return (
        jax.ShapeDtypeStruct((2, sp, d), F32),
        jax.ShapeDtypeStruct((4, 2, sp, d), BF),
        jax.ShapeDtypeStruct((1, d), F32),
        jax.ShapeDtypeStruct((2, sp, d), BF),
    )


def norm_gather_kernel(h, gain, full, *sems):
    t = lax.axis_index("tensor")

    def finish(j, at, _):
        v = h[j, at].astype(F32)
        full[t, j, at] = (v * inverse_rms(v) * gain[...]).astype(BF)

    run_exchange(h.shape[1], None, finish, full, None, None, None, sems)


def norm_gather(h, gain):
    _, full, _, _ = shapes_of(h)
    return call(norm_gather_kernel, (full,), gather_scratch(h.shape[1]), 0, h, gain)[0]


def plain_gather_kernel(h, full, *sems):
    t = lax.axis_index("tensor")

    def finish(j, at, _):
        full[t, j, at] = h[j, at]

    run_exchange(h.shape[1], None, finish, full, None, None, None, sems)


def plain_gather(h):
    _, full, _, _ = shapes_of(h)
    return call(plain_gather_kernel, (full,), gather_scratch(h.shape[1]), 1, h)[0]


def sum_norm_gather_kernel(rounded, part, h, gain, total, full, got, held, s0, s1, g0, g1):
    t = lax.axis_index("tensor")

    def finish(j, at, term):
        v = h[j, at] + term
        if rounded:
            v = v.astype(BF).astype(F32)
        total[j, at] = v
        full[t, j, at] = (v * inverse_rms(v) * gain[...]).astype(BF)

    run_exchange(h.shape[1], part, finish, full, got, held, (s0, s1), (g0, g1))


def sum_norm_gather(part, h, gain, rounded):
    wide, full, _, _ = shapes_of(h)
    _, sp, d = h.shape
    return call(
        functools.partial(sum_norm_gather_kernel, rounded),
        (wide, full),
        scatter_scratch(sp, d) + gather_scratch(sp),
        2 + rounded,
        part, h, gain,
    )


def sum_only_kernel(part, h, total, got, held, s0, s1):
    def finish(j, at, term):
        total[j, at] = (h[j, at] + term).astype(BF)

    run_exchange(h.shape[1], part, finish, None, got, held, (s0, s1), None)


def sum_only(part, h):
    _, _, _, narrow = shapes_of(h)
    _, sp, d = h.shape
    return call(sum_only_kernel, (narrow,), scatter_scratch(sp, d), 4, part, h)[0]


def back_kernel(kind, part, h, gain, g, *refs):
    t = lax.axis_index("tensor")
    if kind == 2:
        dv_out, dgain, got, held, s0, s1 = refs
        full = ga = None
    else:
        dv_out, dgain, full, got, held, s0, s1, g0, g1 = refs
        ga = (g0, g1)
    dgain[...] = jnp.zeros_like(dgain)

    def finish(j, at, term):
        dv, dg = norm_back(h[j, at], gain[...], term)
        dgain[...] += dg
        dv = dv + g[j, at].astype(F32)
        dv_out[j, at] = dv.astype(dv_out.dtype)
        if full is not None:
            full[t, j, at] = dv.astype(BF)

    run_exchange(h.shape[1], part, finish, full, got, held, (s0, s1), ga)


def back(part, h, gain, g, kind):
    wide, full, row, narrow = shapes_of(h)
    _, sp, d = h.shape
    out = (narrow if kind == 1 else wide, row)
    scratch = scatter_scratch(sp, d)
    if kind != 2:
        out += (full,)
        scratch += gather_scratch(sp)
    return call(
        functools.partial(back_kernel, kind), out, scratch, 5 + kind, part, h, gain, g
    )


def turn_matrix(heads, total):
    half = HEAD_DIM // 2
    m = np.zeros((total, total), np.float32)
    for h in range(heads):
        at = h * HEAD_DIM
        for i in range(half):
            m[at + half + i, at + i] = -1.0
            m[at + i, at + half + i] = 1.0
    return m


def swap(value):
    return lax.ppermute(value, "section", [(0, 1), (1, 0)])


def on_device(
    inputs, cotangent, block_order, attn_gain, w_query, key_weight, value_weight, w_out,
    mlp_gain, w_gate, w_up, w_down,
):
    sec = lax.axis_index("section")
    first = sec == 0
    ctx = lax.axis_index("ctx")
    n_t = lax.axis_size("tensor")
    n_ctx = lax.axis_size("ctx")
    _, _, _, sp, half_width = inputs.shape
    length = sp * n_t
    d = 2 * half_width
    rows = n_t * 2 * sp
    wq, wk, wv = w_query[0], key_weight[0], value_weight[0]
    q_w, kv_w = wq.shape[1], 2 * wk.shape[1]
    qkv_w = q_w + kv_w
    q_heads, kv_heads = q_w // HEAD_DIM, kv_w // (2 * HEAD_DIM)

    def to_own(x):
        keep = lax.dynamic_index_in_dim(x[:, 0], sec, 0, keepdims=False)
        give = lax.dynamic_index_in_dim(x[:, 0], 1 - sec, 0, keepdims=False)
        got = swap(give)
        return jnp.where(
            first, jnp.concatenate([keep, got], -1), jnp.concatenate([got, keep], -1)
        )

    def from_own(y, out_dtype):
        lo, hi = y[..., :half_width], y[..., half_width:]
        keep = jnp.where(first, lo, hi)
        got = swap(jnp.where(first, hi, lo).astype(BF)).astype(y.dtype)
        return jnp.where(first, jnp.stack([keep, got]), jnp.stack([got, keep]))[
            :, None
        ].astype(out_dtype)

    x_own = to_own(inputs)
    g_own = to_own(cotangent)

    turn_q = jnp.asarray(turn_matrix(q_heads, q_w), BF)
    turn_kv = turn_matrix(kv_heads, kv_w)
    wkv = jnp.concatenate([wk, wv], 1)
    wcat = jnp.concatenate(
        [wq, wkv, nn(wq, turn_q).astype(BF), nn(wkv, jnp.asarray(turn_kv, BF)).astype(BF)], 1
    )

    def both(w):
        return lax.all_gather(w, "section", axis=0)

    wcat2, wo2, wg2, wu2, wd2, gains2 = (
        both(wcat), both(w_out[0]), both(w_gate[0]), both(w_up[0]), both(w_down[0]),
        both(jnp.concatenate([attn_gain, mlp_gain], 0)),
    )

    own = lax.dynamic_slice_in_dim(block_order, 2 * ctx, 2, 0)
    offs = jnp.arange(length, dtype=jnp.int32)
    pos = own[:, None] * length + offs[None, :]
    freq = ROPE_BASE ** (-(jnp.arange(0, HEAD_DIM, 2).astype(F32) / HEAD_DIM))
    phase_t = freq[None, :, None] * pos.astype(F32)[:, None, :]
    phase_t = jnp.concatenate([phase_t, phase_t], 1)
    cos_t, sin_t = jnp.cos(phase_t), jnp.sin(phase_t)

    def rows_of(t):
        t = jnp.swapaxes(t, 1, 2).reshape(2, n_t, sp, HEAD_DIM)
        return jnp.swapaxes(t, 0, 1).reshape(rows, HEAD_DIM)

    cos_r, sin_r = rows_of(cos_t), rows_of(sin_t)
    ones = jnp.ones((rows, kv_w // 2), F32)
    cos_kv = jnp.concatenate([jnp.tile(cos_r, (1, kv_heads)), ones], 1)
    sin_kv = jnp.concatenate([jnp.tile(sin_r, (1, kv_heads)), 0 * ones], 1)
    cos_all = jnp.concatenate([jnp.tile(cos_r, (1, q_heads)), cos_kv], 1)
    sin_all = jnp.concatenate([jnp.tile(sin_r, (1, q_heads)), sin_kv], 1)

    def gain_of(layer, kind):
        return gains2[layer, kind : kind + 1]

    def attend(n1, layer):
        raw = nn(n1, wcat2[layer])
        qkv = (raw[:, :qkv_w] * cos_all + raw[:, qkv_w:] * sin_all).astype(BF)
        q = qkv[:, :q_w].reshape(n_t, 2, sp, q_w)
        kv = lax.all_gather(qkv[:, q_w:].reshape(n_t, 2, sp, kv_w), "ctx", axis=0)
        mix, mixt, lse = flash_forward(block_order, own, q, kv)
        part = nn(mix.reshape(rows, q_w), wo2[layer]).astype(BF)
        return part.reshape(n_t, 2, sp, d), (q, kv, mix.reshape(rows, q_w), mixt, lse)

    def feed(n2, layer):
        gate, up = nn(n2, wg2[layer]), nn(n2, wu2[layer])
        act = silu_product(gate, up).astype(BF)
        part = nn(act, wd2[layer]).astype(BF)
        return part.reshape(n_t, 2, sp, d), (gate, up, act)

    def feed_back(gm, layer, kept):
        gate, up, _ = kept
        dact = nt(gm, wd2[layer])
        _, pull = jax.vjp(silu_product, gate, up)
        dgate, dup = pull(dact)
        dgate, dup = dgate.astype(BF), dup.astype(BF)
        part = (nt(dgate, wg2[layer]) + nt(dup, wu2[layer])).astype(BF)
        return part.reshape(n_t, 2, sp, d), dgate, dup

    def attend_back(ga, layer, kept):
        q, kv, _, mixt, lse = kept
        dmix = nt(ga, wo2[layer]).astype(BF)
        dq, dkv = flash_backward(
            block_order, own, q, kv, dmix.reshape(n_t, 2, sp, q_w), mixt, lse, cos_t, sin_t
        )
        dkv = lax.psum_scatter(dkv, "ctx", scatter_dimension=0).astype(F32).reshape(rows, kv_w)
        turned = lax.dot_general(
            dkv * sin_kv,
            jnp.asarray(-turn_kv),
            (((1,), (0,)), ((), ())),
            precision=lax.Precision.HIGHEST,
            preferred_element_type=F32,
        )
        dkv = (dkv * cos_kv + turned).astype(BF)
        dqkv = jnp.concatenate([dq.reshape(rows, q_w), dkv], 1)
        part = nt(dqkv, wcat2[layer][:, :qkv_w]).astype(BF)
        return part.reshape(n_t, 2, sp, d), dqkv

    def halve(g):
        size = g.shape[0] // 2
        give = lax.dynamic_slice_in_dim(g, (1 - sec) * size, size, 0).astype(BF)
        keep = lax.dynamic_slice_in_dim(g, sec * size, size, 0)
        return (keep + swap(give).astype(F32)).astype(BF)

    def over_ctx(*grads, after=None):
        halves = tuple(halve(g) for g in grads)
        if after is not None:
            halves, _ = lax.optimization_barrier((halves, after))
        return lax.psum(halves, "ctx")

    flat = lambda v: v.reshape(rows, d)
    a0, a1, m0, m1 = gain_of(0, 0), gain_of(1, 0), gain_of(0, 1), gain_of(1, 1)

    h0 = x_own.astype(F32)
    n1_0 = flat(norm_gather(x_own, a0))
    part, att0 = attend(n1_0, 0)
    h2_0, full = sum_norm_gather(part, h0, m0, False)
    n2_0 = flat(full)
    part, mlp0 = feed(n2_0, 0)
    h1, full = sum_norm_gather(part, h2_0, a1, True)
    n1_1 = flat(full)
    part, att1 = attend(n1_1, 1)
    h2_1, full = sum_norm_gather(part, h1, m1, False)
    n2_1 = flat(full)
    part, mlp1 = feed(n2_1, 1)
    y = sum_only(part, h2_1)

    gm1 = flat(plain_gather(g_own))
    part, dgate1, dup1 = feed_back(gm1, 1, mlp1)
    dh2_1, dm1, full = back(part, h2_1, m1, g_own.astype(F32), 0)
    ga1 = flat(full)
    part, dqkv1 = attend_back(ga1, 1, att1)
    g0, da1, full = back(part, h1, a1, dh2_1, 1)
    gm0 = flat(full)
    grads1 = over_ctx(
        tn(mlp1[2], gm1), tn(n2_1, dgate1), tn(n2_1, dup1), tn(att1[2], ga1), tn(n1_1, dqkv1)
    )
    part, dgate0, dup0 = feed_back(gm0, 0, mlp0)
    dh2_0, dm0, full = back(part, h2_0, m0, g0.astype(F32), 0)
    ga0 = flat(full)
    grads0 = over_ctx(tn(mlp0[2], gm0), tn(n2_0, dgate0), tn(n2_0, dup0), after=grads1)
    part, dqkv0 = attend_back(ga0, 0, att0)
    dh0, da0 = back(part, h0, a0, dh2_0, 2)
    grads0 += over_ctx(tn(att0[2], ga0), tn(n1_0, dqkv0), after=grads0)
    gains0, gains1 = (da0, dm0), (da1, dm1)

    gain_sum = lax.psum(jnp.stack([jnp.concatenate(gains0), jnp.concatenate(gains1)]), ("section", "ctx", "tensor"))
    gain_own = lax.dynamic_index_in_dim(gain_sum, sec, 0, keepdims=False)

    def to_owner(r0, r1):
        got = swap(jnp.where(first, r1, r0))
        keep = jnp.where(first, r0, r1)
        return jnp.where(
            first, jnp.concatenate([keep, got], 0), jnp.concatenate([got, keep], 0)
        ).astype(F32)

    gd, gg, gu, go, gqkv = (to_owner(a, b) for a, b in zip(grads0, grads1))
    half_kv = kv_w // 2
    return (
        from_own(y, BF),
        from_own(dh0, F32),
        gain_own[0:1],
        gqkv[None, :, :q_w],
        gqkv[None, :, q_w : q_w + half_kv],
        gqkv[None, :, q_w + half_kv :],
        go[None],
        gain_own[1:2],
        gg[None],
        gu[None],
        gd[None],
    )


def solution(mesh):
    rows = P(None, "ctx", None, "tensor", "section")
    gain = P("section", None)
    col = P("section", None, "tensor")
    row = P("section", "tensor", None)
    return jax.shard_map(
        on_device,
        mesh=mesh,
        in_specs=(rows, rows, P(), gain, col, col, col, row, gain, col, col, row),
        out_specs=(rows, rows, gain, col, col, col, row, gain, col, col, row),
        check_vma=False,
    )
```

```python
import functools

import jax
import jax.numpy as jnp
import numpy as np
from jax import lax
from jax.experimental import pallas as pl
from jax.experimental.pallas import tpu as pltpu
from jax.sharding import PartitionSpec as P

HEAD_DIM = 96
EPSILON = 1e-05
ROPE_BASE = 100000.0
LOG2E = 1.4426950408889634
BF = jnp.bfloat16
F32 = jnp.float32


def nn(a, b):
    return lax.dot_general(a, b, (((1,), (0,)), ((), ())), preferred_element_type=F32)


def nt(a, b):
    return lax.dot_general(a, b, (((1,), (1,)), ((), ())), preferred_element_type=F32)


def tn(a, b):
    return lax.dot_general(a, b, (((0,), (0,)), ((), ())), preferred_element_type=F32)


def head_of(x, h):
    return x[:, h * HEAD_DIM : (h + 1) * HEAD_DIM]


def transposed(x):
    return x.astype(F32).T.astype(BF)


def causal(length):
    keys = lax.broadcasted_iota(jnp.int32, (length, length), 0)
    queries = lax.broadcasted_iota(jnp.int32, (length, length), 1)
    return keys <= queries


def silu_product(gate, up):
    return gate * jax.nn.sigmoid(gate) * up


MESH = pl.DeviceIdType.MESH


def tensor_peers():
    t = lax.axis_index("tensor")
    return t, t + 1 - 2 * lax.rem(t, 2), lax.rem(t + 2, 4), 3 - t


def greet(tensor=True, line=False, after=False):
    barrier = pltpu.get_barrier_semaphore()
    count = 0
    if tensor:
        _, x, y, _ = tensor_peers()
        for peer in (x, y):
            pl.semaphore_signal(barrier, inc=1, device_id={"tensor": peer}, device_id_type=MESH)
        count += 2
    if line:
        c, _, has_left, has_right = ctx_ends()
        for there, peer in ((has_left, c - 1), (has_right, c + 1)):

            @pl.when(there)
            def _():
                pl.semaphore_signal(
                    barrier, inc=1, device_id={"ctx": peer}, device_id_type=MESH
                )

        count += has_left.astype(jnp.int32) + has_right.astype(jnp.int32)
    if after:
        count += lax.axis_index("section")
    pl.semaphore_wait(barrier, count)


def send(src, dst, sems, at, peer):
    return pltpu.make_async_remote_copy(
        src_ref=src,
        dst_ref=dst,
        send_sem=sems[0].at[at],
        recv_sem=sems[1].at[at],
        device_id={"tensor": peer},
        device_id_type=MESH,
    )


def gather_start(full, sems, chunks, q):
    t, x, y, _ = tensor_peers()
    j, at = chunks[q]
    near, far = (x, y) if j == 0 else (y, x)
    own = full.at[t, j, at]
    send(own, own, sems, (q, 0), near).start()
    send(own, own, sems, (q, 1), far).start()


def gather_pass(full, sems, chunks, q):
    _, x, y, _ = tensor_peers()
    j, at = chunks[q]
    near, far = (x, y) if j == 0 else (y, x)
    got = full.at[near, j, at]
    send(got, got, sems, (q, 0), near).wait_recv()
    send(got, got, sems, (q, 2), far).start()


def gather_end(full, sems, chunks, q):
    t, x, y, diag = tensor_peers()
    j, at = chunks[q]
    near, far = (x, y) if j == 0 else (y, x)
    for kind, owner in ((1, far), (2, diag)):
        got = full.at[owner, j, at]
        send(got, got, sems, (q, kind), far).wait_recv()


def gather_drain(full, sems, chunks, q):
    t, x, _, _ = tensor_peers()
    j, at = chunks[q]
    own = full.at[t, j, at]
    for kind in range(3):
        send(own, own, sems, (q, kind), x).wait_send()


def scatter_start(part, got, sems, chunks, q):
    _, x, y, diag = tensor_peers()
    j, at = chunks[q]
    far = y if j == 0 else x
    send(part.at[diag, j, at], got.at[0, j, at], sems, (q, 0), far).start()
    send(part.at[far, j, at], got.at[2, j, at], sems, (q, 2), far).start()


def scatter_pass(part, got, held, sems, chunks, q):
    _, x, y, _ = tensor_peers()
    j, at = chunks[q]
    near = x if j == 0 else y
    send(held.at[j, at], got.at[0, j, at], sems, (q, 0), near).wait_recv()
    held[j, at] = (part[near, j, at].astype(F32) + got[0, j, at].astype(F32)).astype(BF)
    send(held.at[j, at], got.at[1, j, at], sems, (q, 1), near).start()


def scatter_end(part, got, held, sems, chunks, q):
    t, x, _, _ = tensor_peers()
    j, at = chunks[q]
    for kind in (2, 1):
        send(held.at[j, at], got.at[kind, j, at], sems, (q, kind), x).wait_recv()
    return (
        part[t, j, at].astype(F32) + got[1, j, at].astype(F32) + got[2, j, at].astype(F32)
    )


def scatter_drain(part, got, sems, chunks, q):
    t, x, _, _ = tensor_peers()
    j, at = chunks[q]
    for kind in range(3):
        send(part.at[t, j, at], got.at[kind, j, at], sems, (q, kind), x).wait_send()


def inverse_rms(v):
    return lax.rsqrt(jnp.mean(v * v, axis=-1, keepdims=True) + EPSILON)


def norm_back(v, gain, dn):
    r = inverse_rms(v)
    unit = v * r
    scaled = dn * gain
    dv = r * (scaled - unit * jnp.mean(scaled * unit, axis=-1, keepdims=True))
    return dv, jnp.sum((dn * unit).reshape(-1, 8, v.shape[-1]), axis=0)


def chunk_list(sp):
    parts = 2
    size = sp // parts
    return [(j, pl.ds(s * size, size)) for s in range(parts) for j in range(2)]


def run_exchange(
    sp, part, finish, full, got, held, sc_sems, ga_sems,
    between=None, after=None, chain=None, turns=False,
):
    chunks = chunk_list(sp)
    n = range(len(chunks))
    greet(line=chain is not None, after=turns)
    steps = []
    if part is not None:
        for q in n:
            scatter_start(part, got, sc_sems, chunks, q)
        steps += [
            functools.partial(scatter_pass, part, got, held, sc_sems, chunks, q) for q in n
        ]

    def end(q):
        j, at = chunks[q]
        total = None if part is None else scatter_end(part, got, held, sc_sems, chunks, q)
        finish(j, at, total)
        if full is not None:
            gather_start(full, ga_sems, chunks, q)

    steps += [functools.partial(end, q) for q in n]
    if between is not None:
        steps.append(between)
    if full is not None:
        steps += [functools.partial(gather_pass, full, ga_sems, chunks, q) for q in n]
    if after is not None:
        steps.append(after)
    if full is not None:
        steps += [functools.partial(gather_end, full, ga_sems, chunks, q) for q in n]
    if chain is None:
        for step in steps:
            step()
    else:
        done = 0
        for time in range(chain.slots):
            chain.slot(time)
            goal = min(len(steps), int(len(steps) * (time + 1) / (0.8 * chain.slots)))
            for step in steps[done:goal]:
                step()
            done = goal
        for step in steps[done:]:
            step()
        chain.drain()
    if turns:

        @pl.when(lax.axis_index("section") == 0)
        def _():
            pl.semaphore_signal(
                pltpu.get_barrier_semaphore(),
                inc=1,
                device_id={"section": 1},
                device_id_type=MESH,
            )

    if full is not None:
        for q in n:
            gather_drain(full, ga_sems, chunks, q)
    if part is not None:
        for q in n:
            scatter_drain(part, got, sc_sems, chunks, q)


class Chain:
    def __init__(self, zs, gots, outs, sems):
        self.zs, self.gots, self.outs = zs, gots, outs
        self.sum_sems, self.back_sems = sems[:2], sems[2:]
        self.c, self.n, _, _ = ctx_ends()
        self.starts = [sum(z.shape[1] for z in zs[:k]) for k in range(len(zs))]
        self.hop = 2
        self.slots = sum(z.shape[1] for z in zs) + 2 * self.hop * (self.n - 1)

    def copy(self, src, dst, sems, d, k, i, peer):
        at = self.starts[k] + i
        return along(src[k].at[d, i], dst[k].at[d, i], sems[0].at[d, at], sems[1].at[d, at], peer)

    def sides(self, d):
        c, n = self.c, self.n
        return (c, c + 1, c - 1) if d == 0 else (n - 1 - c, c - 1, c + 1)

    def slot(self, time):
        n, zs, gots, outs = self.n, self.zs, self.gots, self.outs
        for d in range(2):
            place, ahead, behind = self.sides(d)
            due = time - self.hop * place
            due_back = time - self.hop * (2 * (n - 1) - place)
            for k in range(len(zs)):
                i = due - self.starts[k]
                going = (i >= 0) & (i < zs[k].shape[1])

                @pl.when(going & (place == 0))
                def _():
                    self.copy(zs, gots, self.sum_sems, d, k, i, ahead).start()

                @pl.when(going & (place > 0))
                def _():
                    self.copy(zs, gots, self.sum_sems, d, k, i, ahead).wait_recv()
                    total = (gots[k][d, i].astype(F32) + zs[k][d, i].astype(F32)).astype(BF)

                    @pl.when(place < n - 1)
                    def _():
                        gots[k][d, i] = total
                        self.copy(gots, gots, self.sum_sems, d, k, i, ahead).start()

                    @pl.when(place == n - 1)
                    def _():
                        outs[k][d, i] = total
                        self.copy(outs, outs, self.back_sems, d, k, i, behind).start()

                i_back = due_back - self.starts[k]
                coming = (i_back >= 0) & (i_back < zs[k].shape[1]) & (place < n - 1)

                @pl.when(coming)
                def _():
                    self.copy(outs, outs, self.back_sems, d, k, i_back, behind).wait_recv()

                    @pl.when(place > 0)
                    def _():
                        self.copy(outs, outs, self.back_sems, d, k, i_back, behind).start()

    def drain(self):
        for d in range(2):
            place, ahead, behind = self.sides(d)
            for k in range(len(self.zs)):

                def one(i, _):
                    @pl.when(place < self.n - 1)
                    def _():
                        self.copy(self.zs, self.gots, self.sum_sems, d, k, i, ahead).wait_send()

                    @pl.when(place > 0)
                    def _():
                        self.copy(
                            self.outs, self.outs, self.back_sems, d, k, i, behind
                        ).wait_send()

                    return 0

                lax.fori_loop(0, self.zs[k].shape[1], one, 0)


def chain_scratch(zs):
    sems = pltpu.SemaphoreType.DMA((2, sum(z.shape[1] for z in zs)))
    return [pltpu.VMEM(z.shape, BF) for z in zs] + [sems] * 4


def scatter_scratch(sp, d):
    n = len(chunk_list(sp))
    return [
        pltpu.VMEM((3, 2, sp, d), BF),
        pltpu.VMEM((2, sp, d), BF),
        pltpu.SemaphoreType.DMA((n, 3)),
        pltpu.SemaphoreType.DMA((n, 3)),
    ]


def gather_scratch(sp):
    n = len(chunk_list(sp))
    return [pltpu.SemaphoreType.DMA((n, 3)), pltpu.SemaphoreType.DMA((n, 3))]


def call(kernel, out_shape, scratch, ident, *operands):
    vm = pl.BlockSpec(memory_space=pltpu.VMEM)
    return pl.pallas_call(
        kernel,
        out_shape=out_shape,
        in_specs=[vm] * len(operands),
        out_specs=(vm,) * len(out_shape),
        scratch_shapes=scratch,
        compiler_params=pltpu.CompilerParams(
            collective_id=ident, has_side_effects=True, vmem_limit_bytes=50 * 2**20
        ),
    )(*operands)


def shapes_of(h):
    _, sp, d = h.shape
    return (
        jax.ShapeDtypeStruct((2, sp, d), F32),
        jax.ShapeDtypeStruct((4, 2, sp, d), BF),
        jax.ShapeDtypeStruct((1, d), F32),
        jax.ShapeDtypeStruct((2, sp, d), BF),
    )


def norm_gather_kernel(h, gain, full, *sems):
    t = lax.axis_index("tensor")

    def finish(j, at, _):
        v = h[j, at].astype(F32)
        full[t, j, at] = (v * inverse_rms(v) * gain[...]).astype(BF)

    run_exchange(h.shape[1], None, finish, full, None, None, None, sems)


def norm_gather(h, gain):
    _, full, _, _ = shapes_of(h)
    return call(norm_gather_kernel, (full,), gather_scratch(h.shape[1]), 0, h, gain)[0]


def sum_norm_gather_kernel(kind, part, h, gain, total, full, got, held, s0, s1, g0, g1):
    t = lax.axis_index("tensor")

    def finish(j, at, term):
        v = h[j, at] + term
        if kind == 1:
            v = v.astype(BF).astype(F32)
        total[j, at] = v
        full[t, j, at] = (v * inverse_rms(v) * gain[...]).astype(BF)

    run_exchange(
        h.shape[1], part, finish, full, got, held, (s0, s1), (g0, g1), turns=kind == 0
    )


def sum_norm_gather(part, h, gain, kind):
    wide, full, _, _ = shapes_of(h)
    _, sp, d = h.shape
    return call(
        functools.partial(sum_norm_gather_kernel, kind),
        (wide, full),
        scatter_scratch(sp, d) + gather_scratch(sp),
        2 + kind,
        part, h, gain,
    )


def line_sum(own, rows, sems):
    c, _, has_left, has_right = ctx_ends()
    sides = ((has_left, has_right, c + 1, 0), (has_right, has_left, c - 1, 1))
    for come, go, ahead, d in sides:
        copy = along(rows.at[2 * d + 1], rows.at[2 * d], sems[0].at[d], sems[1].at[d], ahead)
        rows[2 * d + 1] = own

        @pl.when(come)
        def _():
            copy.wait_recv()
            rows[2 * d + 1] = own + rows[2 * d]

        @pl.when(go)
        def _():
            copy.start()

    total = own
    for come, go, ahead, d in sides:
        copy = along(rows.at[2 * d + 1], rows.at[2 * d], sems[0].at[d], sems[1].at[d], ahead)
        total = total + jnp.where(come, rows[2 * d], 0.0)

        @pl.when(go)
        def _():
            copy.wait_send()

    return total


def back_kernel(kind, count, *refs):
    refs = list(refs)

    def take(size):
        out = refs[:size]
        del refs[:size]
        return out

    t, x, y, _ = tensor_peers()
    part, h, gain, g = take(4)
    others = take(1)[0] if kind == 2 else None
    zs = take(count)
    dv_out, dgain = take(2)
    z_out = take(count)
    full = take(1)[0] if kind != 2 else None
    got, held, s0, s1, rows, gs, gr = take(7)
    z_got = take(count)
    z_sems = take(4)
    ga = take(2) if kind != 2 else None
    line = take(3) if kind == 2 else None
    chain = Chain(zs, z_got, z_out, z_sems)
    rows[0] = jnp.zeros_like(rows[0])

    def finish(j, at, term):
        dv, dg = norm_back(h[j, at], gain[...], term)
        rows[0] = rows[0] + dg
        dv = dv + g[j, at].astype(F32)
        dv_out[j, at] = dv.astype(dv_out.dtype)
        if full is not None:
            full[t, j, at] = dv.astype(BF)

    def add_gains(step, peer):
        send(rows.at[2 * step], rows.at[2 * step + 1], (gs, gr), step, peer).start()

    def end_gains(step, peer):
        send(rows.at[2 * step], rows.at[2 * step + 1], (gs, gr), step, peer).wait()

    def between():
        add_gains(0, x)

    def after():
        end_gains(0, x)
        rows[2] = rows[0] + rows[1]
        add_gains(1, y)

    run_exchange(
        h.shape[1], part, finish, full, got, held, (s0, s1), ga, between, after, chain
    )
    end_gains(1, y)
    total = jnp.sum(rows[2] + rows[3], axis=0, keepdims=True)
    if kind == 2:
        blank = jnp.zeros((4, total.shape[1]), F32)
        total = jnp.concatenate([total, others[...], blank], axis=0)
        dgain[...] = line_sum(total, line[0], line[1:])
    else:
        dgain[...] = total


def back(part, h, gain, g, kind, zs, others=None):
    wide, full, row, narrow = shapes_of(h)
    _, sp, d = h.shape
    row = jax.ShapeDtypeStruct((8, d), F32) if kind == 2 else row
    out = (narrow if kind == 1 else wide, row)
    out += tuple(jax.ShapeDtypeStruct(z.shape, BF) for z in zs)
    scratch = scatter_scratch(sp, d) + [
        pltpu.VMEM((4, 8, d), F32),
        pltpu.SemaphoreType.DMA((2,)),
        pltpu.SemaphoreType.DMA((2,)),
    ] + chain_scratch(zs)
    if kind != 2:
        out += (full,)
        scratch += gather_scratch(sp)
    else:
        scratch += [
            pltpu.VMEM((4, 8, d), F32),
            pltpu.SemaphoreType.DMA((2,)),
            pltpu.SemaphoreType.DMA((2,)),
        ]
    operands = (part, h, gain, g) + (() if others is None else (others,)) + tuple(zs)
    res = call(
        functools.partial(back_kernel, kind, len(zs)), out, scratch, 5 + kind, *operands
    )
    return res[0], res[1], res[2 : 2 + len(zs)], res[2 + len(zs) :]


def ctx_ends():
    c = lax.axis_index("ctx")
    n = lax.axis_size("ctx")
    return c, n, c > 0, c < n - 1


def along(src, dst, send_sem, recv_sem, peer):
    return pltpu.make_async_remote_copy(
        src_ref=src,
        dst_ref=dst,
        send_sem=send_sem,
        recv_sem=recv_sem,
        device_id={"ctx": peer},
        device_id_type=MESH,
    )


def fwd_kernel(extra, *refs):
    if extra:
        (
            qkv_ref, h_ref, mix_ref, mixt_ref, lse_ref, kv_all, full,
            qt, m_s, l_s, acc, to_left, to_right, arrive, *ga,
        ) = refs
    else:
        (
            qkv_ref, mix_ref, mixt_ref, lse_ref, kv_all,
            qt, m_s, l_s, acc, to_left, to_right, arrive,
        ) = refs
    c, n, has_left, has_right = ctx_ends()
    n_t, _, sp, _ = qkv_ref.shape
    length, width = kv_all.shape[2:]
    kv_heads = width // (2 * HEAD_DIM)
    q_heads = qt.shape[1]
    q_w = q_heads * HEAD_DIM
    group = q_heads // kv_heads
    scale = HEAD_DIM**-0.5 * LOG2E

    def leftward(r, j):
        at = kv_all.at[r, j]
        return along(at, at, to_left.at[r, j], arrive.at[r, j], c - 1)

    def rightward(r):
        at = kv_all.at[r, 0]
        return along(at, at, to_right.at[r], arrive.at[r, 0], c + 1)

    def pass_left(r):
        @pl.when(has_left)
        def _():
            leftward(r, 0).start()
            leftward(r, 1).start()

    def pass_right(r):
        @pl.when(has_right)
        def _():
            rightward(r).start()

    for j in range(2):
        kv_all[c, j] = qkv_ref[:, j, :, q_w:].reshape(length, width)
    if extra:
        chunks = chunk_list(sp)
        t, _, _, _ = tensor_peers()

    greet(tensor=extra, line=True)
    pass_left(c)
    pass_right(c)
    if extra:
        for q in range(len(chunks)):
            j, at = chunks[q]
            full[t, j, at] = h_ref[j, at]
            gather_start(full, ga, chunks, q)

    for j in range(2):
        x = qkv_ref[:, j, :, :q_w].reshape(length, q_w)
        for h in range(q_heads):
            qt[j, h] = transposed(head_of(x, h))
    m_s[...] = jnp.full_like(m_s, -1e30)
    l_s[...] = jnp.zeros_like(l_s)
    acc[...] = jnp.zeros_like(acc)

    def pair(r, kj, j, masked):
        x = kv_all[r, kj]
        for h in range(q_heads):
            s = nn(head_of(x, h // group), qt[j, h]) * scale
            if masked:
                s = jnp.where(causal(length), s, -1e30)
            m_old = m_s[j, h]
            m_new = jnp.maximum(m_old, jnp.max(s, axis=0, keepdims=True))
            alpha = jnp.exp2(m_old - m_new)
            p = jnp.exp2(s - m_new)
            l_s[j, h] = l_s[j, h] * alpha + jnp.sum(p, axis=0, keepdims=True)
            m_s[j, h] = m_new
            value = transposed(head_of(x, kv_heads + h // group))
            acc[j, h] = acc[j, h] * alpha + nn(value, p.astype(BF))

    def diagonal(j, _):
        pair(c, j, j, True)
        return 0

    lax.fori_loop(0, 2, diagonal, 0)
    if extra:
        for q in range(len(chunks)):
            gather_pass(full, ga, chunks, q)

    def step(s, _):
        from_right = (s > 0) & (c + s < n)
        from_left = (s > 0) & (c - s >= 0)

        @pl.when(from_right)
        def _():
            leftward(c + s, 0).wait_recv()
            leftward(c + s, 1).wait_recv()
            pass_left(c + s)

        @pl.when(from_left)
        def _():
            rightward(c - s).wait_recv()
            pass_right(c - s)

        def item(i, _):
            side = i // 2
            k = lax.rem(i, 2)
            r = jnp.where(side == 0, c + s, c - s)
            ready = jnp.where(side == 0, from_right, from_left) | ((s == 0) & (i == 0))

            @pl.when(ready)
            def _():
                pair(r, jnp.where(side == 0, k, 0), jnp.where(side == 0, 1, k), False)

            return 0

        lax.fori_loop(0, 4, item, 0)
        return 0

    lax.fori_loop(0, n, step, 0)
    for j in range(2):
        outs = []
        for h in range(q_heads):
            out = acc[j, h] / l_s[j, h]
            mixt_ref[j, h] = out.astype(BF)
            lse_ref[j, h] = m_s[j, h] + jnp.log2(l_s[j, h])
            outs.append(out.T)
        mix_ref[:, j] = jnp.concatenate(outs, axis=-1).astype(BF).reshape(n_t, sp, -1)

    def drain(r, _):
        @pl.when((r >= c) & has_left)
        def _():
            leftward(r, 0).wait_send()
            leftward(r, 1).wait_send()

        @pl.when((r <= c) & has_right)
        def _():
            rightward(r).wait_send()

        return 0

    lax.fori_loop(0, n, drain, 0)
    if extra:
        for q in range(len(chunks)):
            gather_end(full, ga, chunks, q)
        for q in range(len(chunks)):
            gather_drain(full, ga, chunks, q)


def flash_forward(qkv, q_heads, h=None):
    n_t, _, sp, width = qkv.shape
    n = lax.axis_size("ctx")
    q_w = q_heads * HEAD_DIM
    length = n_t * sp
    rows = (2, q_heads, 1, length)
    cols = (2, q_heads, HEAD_DIM, length)
    extra = h is not None
    return call(
        functools.partial(fwd_kernel, extra),
        (
            jax.ShapeDtypeStruct((n_t, 2, sp, q_w), BF),
            jax.ShapeDtypeStruct(cols, BF),
            jax.ShapeDtypeStruct(rows, F32),
            jax.ShapeDtypeStruct((n, 2, length, width - q_w), BF),
        )
        + ((shapes_of(h)[1],) if extra else ()),
        [
            pltpu.VMEM(cols, BF),
            pltpu.VMEM(rows, F32),
            pltpu.VMEM(rows, F32),
            pltpu.VMEM(cols, F32),
            pltpu.SemaphoreType.DMA((n, 2)),
            pltpu.SemaphoreType.DMA((n,)),
            pltpu.SemaphoreType.DMA((n, 2)),
        ]
        + (gather_scratch(sp) if extra else []),
        9 if extra else 10,
        qkv,
        *((h,) if extra else ()),
    )


def bwd_kernel(extra, *refs):
    if extra:
        (
            qkv_ref, kv_all, do_ref, mixt_ref, lse_ref, cos_ref, sin_ref, cos_n, sin_n,
            part_ref, h_ref, out_ref, y_ref,
            qt, dot, qn, don, dl_s, dqt, acc, got_r, got_l, put_r, put_l, sr, ar, sl, al,
            sc_got, sc_held, *sc,
        ) = refs
    else:
        (
            qkv_ref, kv_all, do_ref, mixt_ref, lse_ref, cos_ref, sin_ref, cos_n, sin_n, out_ref,
            qt, dot, qn, don, dl_s, dqt, acc, got_r, got_l, put_r, put_l, sr, ar, sl, al,
        ) = refs
    c, n, has_left, has_right = ctx_ends()
    n_t, _, sp, _ = qkv_ref.shape
    length, width = kv_all.shape[2:]
    kv_heads = width // (2 * HEAD_DIM)
    q_heads = qt.shape[1]
    q_w = q_heads * HEAD_DIM
    group = q_heads // kv_heads
    scale = HEAD_DIM**-0.5
    half = HEAD_DIM // 2

    def rightward(r):
        return along(put_r.at[r], got_r.at[r], sr.at[r], ar.at[r], c + 1)

    def leftward(r):
        return along(put_l.at[r], got_l.at[r], sl.at[r], al.at[r], c - 1)

    greet(tensor=extra, line=True)
    if extra:
        chunks = chunk_list(sp)
        for q in range(len(chunks)):
            scatter_start(part_ref, sc_got, sc, chunks, q)
    for j in range(2):
        x = qkv_ref[:, j, :, :q_w].reshape(length, q_w)
        y = do_ref[:, j].reshape(length, q_w)
        for h in range(q_heads):
            a = head_of(x, h)
            qn[j, h] = a
            qt[j, h] = transposed(a)
            b = head_of(y, h)
            don[j, h] = b
            bt = b.astype(F32).T
            dot[j, h] = bt.astype(BF)
            dl_s[j, h] = jnp.sum(bt * mixt_ref[j, h].astype(F32), axis=0, keepdims=True)
    dqt[...] = jnp.zeros_like(dqt)

    def pair(r, kj, j, masked):
        x = kv_all[r, kj]
        for kh in range(kv_heads):
            key = head_of(x, kh)
            value = head_of(x, kv_heads + kh)
            key_t = transposed(key)
            dk = acc[kj, kh]
            dv = acc[kj, kv_heads + kh]
            for g in range(group):
                h = kh * group + g
                s = nn(key, qt[j, h]) * (scale * LOG2E)
                p = jnp.exp2(s - lse_ref[j, h])
                if masked:
                    p = jnp.where(causal(length), p, 0.0)
                dp = nn(value, dot[j, h])
                ds = (p * (dp - dl_s[j, h])).astype(BF)
                dv = dv + nn(p.astype(BF), don[j, h])
                dk = dk + nn(ds, qn[j, h])
                dqt[j, h] += nn(key_t, ds)
            acc[kj, kh] = dk
            acc[kj, kv_heads + kh] = dv

    def joined(kj):
        parts = [acc[kj, i] * (scale if i < kv_heads else 1.0) for i in range(2 * kv_heads)]
        return jnp.concatenate(parts, axis=-1)

    def finish_right(r, has_more):
        @pl.when(has_more)
        def _():
            rightward(r).wait_recv()
            for kj in range(2):
                put_r[r, kj] = (put_r[r, kj].astype(F32) + got_r[r, kj].astype(F32)).astype(BF)

        rightward(r).start()

    def finish_left(r, has_more):
        @pl.when(has_more)
        def _():
            leftward(r).wait_recv()
            put_l[r] = (put_l[r].astype(F32) + got_l[r].astype(F32)).astype(BF)

        leftward(r).start()

    def step(i, _):
        s = n - 1 - i

        def one_side(side, _):
            r = jnp.where(side == 0, c + s, c - s)
            ready = jnp.where(side == 0, c + s < n, (c - s >= 0) & (s > 0))

            @pl.when(ready)
            def _():
                acc[...] = jnp.zeros_like(acc)

                @pl.when(s == 0)
                def _():
                    def diagonal(j, _):
                        pair(c, j, j, True)
                        return 0

                    lax.fori_loop(0, 2, diagonal, 0)

                def item(k, _):
                    @pl.when((s > 0) | (k == 0))
                    def _():
                        pair(r, jnp.where(side == 0, k, 0), jnp.where(side == 0, 1, k), False)

                    return 0

                lax.fori_loop(0, 2, item, 0)

                @pl.when((side == 0) & (s > 0))
                def _():
                    for kj in range(2):
                        put_r[r, kj] = joined(kj).astype(BF)

                    @pl.when(jnp.logical_not(has_left))
                    def _():
                        rightward(r).start()

                @pl.when(side == 1)
                def _():
                    put_l[r] = joined(0).astype(BF)

                    @pl.when(jnp.logical_not(has_right))
                    def _():
                        leftward(r).start()

            return 0

        lax.fori_loop(0, 2, one_side, 0)
        late = s + 1

        @pl.when((c + late < n) & has_left)
        def _():
            finish_right(c + late, has_left)

        @pl.when((c - late >= 0) & has_right)
        def _():
            finish_left(c - late, has_right)

        return 0

    lax.fori_loop(0, 2, step, 0)
    if extra:
        for q in range(len(chunks)):
            scatter_pass(part_ref, sc_got, sc_held, sc, chunks, q)
    lax.fori_loop(2, n, step, 0)
    if extra:
        for q in range(len(chunks)):
            j, at = chunks[q]
            term = scatter_end(part_ref, sc_got, sc_held, sc, chunks, q)
            y_ref[j, at] = (h_ref[j, at] + term).astype(BF)
        for q in range(len(chunks)):
            scatter_drain(part_ref, sc_got, sc, chunks, q)
    for j in range(2):
        outs = []
        for h in range(q_heads):
            d = dqt[j, h] * scale
            sc = d * sin_ref[j]
            back = d * cos_ref[j] + jnp.concatenate([sc[half:], -sc[:half]], axis=0)
            outs.append(back.T)
        out_ref[:, j, :, :q_w] = jnp.concatenate(outs, axis=-1).astype(BF).reshape(n_t, sp, q_w)

    @pl.when(has_right)
    def _():
        leftward(c).wait_recv()

    @pl.when(has_left)
    def _():
        rightward(c).wait_recv()

    for kj in range(2):
        total = joined(kj)
        total += jnp.where(has_left, got_r[c, kj].astype(F32), 0.0)
        if kj == 0:
            total += jnp.where(has_right, got_l[c].astype(F32), 0.0)
        parts = []
        for kh in range(2 * kv_heads):
            d = head_of(total, kh)
            if kh < kv_heads:
                sc = d * sin_n[kj]
                d = d * cos_n[kj] + jnp.concatenate([sc[:, half:], -sc[:, :half]], axis=1)
            parts.append(d)
        out_ref[:, kj, :, q_w:] = jnp.concatenate(parts, axis=-1).astype(BF).reshape(n_t, sp, width)

    def drain(r, _):
        @pl.when((r > c) & has_right)
        def _():
            rightward(r).wait_send()

        @pl.when((r < c) & has_left)
        def _():
            leftward(r).wait_send()

        return 0

    lax.fori_loop(0, n, drain, 0)


def flash_backward(qkv, kv_all, do, mixt, lse, tables, part=None, h=None):
    n, _, length, width = kv_all.shape
    q_heads = mixt.shape[1]
    cols = pltpu.VMEM((2, q_heads, HEAD_DIM, length), BF)
    natural = pltpu.VMEM((2, q_heads, length, HEAD_DIM), BF)
    both = pltpu.VMEM((n, 2, length, width), BF)
    early = pltpu.VMEM((n, length, width), BF)
    sems = pltpu.SemaphoreType.DMA((n,))
    extra = part is not None
    return call(
        functools.partial(bwd_kernel, extra),
        (jax.ShapeDtypeStruct(qkv.shape, BF),) + ((shapes_of(h)[3],) if extra else ()),
        [
            cols,
            cols,
            natural,
            natural,
            pltpu.VMEM((2, q_heads, 1, length), F32),
            pltpu.VMEM((2, q_heads, HEAD_DIM, length), F32),
            pltpu.VMEM((2, width // HEAD_DIM, length, HEAD_DIM), F32),
            both,
            early,
            both,
            early,
            sems,
            sems,
            sems,
            sems,
        ]
        + (scatter_scratch(h.shape[1], h.shape[2]) if extra else []),
        12 if extra else 11,
        qkv, kv_all, do, mixt, lse, *tables, *((part, h) if extra else ()),
    )


def turn_matrix(heads, total):
    half = HEAD_DIM // 2
    m = np.zeros((total, total), np.float32)
    for h in range(heads):
        at = h * HEAD_DIM
        for i in range(half):
            m[at + half + i, at + i] = -1.0
            m[at + i, at + half + i] = 1.0
    return m


def swap(value):
    return lax.ppermute(value, "section", [(0, 1), (1, 0)])


def on_device(
    inputs, cotangent, block_order, attn_gain, w_query, key_weight, value_weight, w_out,
    mlp_gain, w_gate, w_up, w_down,
):
    sec = lax.axis_index("section")
    first = sec == 0
    ctx = lax.axis_index("ctx")
    n_t = lax.axis_size("tensor")
    n_ctx = lax.axis_size("ctx")
    _, _, _, sp, half_width = inputs.shape
    length = sp * n_t
    d = 2 * half_width
    rows = n_t * 2 * sp
    wq, wk, wv = w_query[0], key_weight[0], value_weight[0]
    q_w, kv_w = wq.shape[1], 2 * wk.shape[1]
    qkv_w = q_w + kv_w
    q_heads, kv_heads = q_w // HEAD_DIM, kv_w // (2 * HEAD_DIM)

    def to_own(x):
        keep = lax.dynamic_index_in_dim(x[:, 0], sec, 0, keepdims=False)
        give = lax.dynamic_index_in_dim(x[:, 0], 1 - sec, 0, keepdims=False)
        got = swap(give)
        return jnp.where(
            first, jnp.concatenate([keep, got], -1), jnp.concatenate([got, keep], -1)
        )

    def from_own(y, out_dtype):
        y = in_order(y)
        lo, hi = y[..., :half_width], y[..., half_width:]
        keep = jnp.where(first, lo, hi)
        got = swap(jnp.where(first, hi, lo).astype(BF)).astype(y.dtype)
        return jnp.where(first, jnp.stack([keep, got]), jnp.stack([got, keep]))[
            :, None
        ].astype(out_dtype)

    turned = lax.dynamic_index_in_dim(block_order, 2 * ctx, 0, keepdims=False) != ctx

    def in_order(x):
        return jnp.where(turned, jnp.stack([x[1], x[0]]), x)

    x_own = in_order(to_own(inputs))
    g_own = in_order(to_own(cotangent))

    turn_q = jnp.asarray(turn_matrix(q_heads, q_w), BF)
    turn_kv = turn_matrix(kv_heads, kv_w)
    wkv = jnp.concatenate([wk, wv], 1)
    wcat = jnp.concatenate(
        [wq, wkv, nn(wq, turn_q).astype(BF), nn(wkv, jnp.asarray(turn_kv, BF)).astype(BF)], 1
    )

    def both(w):
        return lax.all_gather(w, "section", axis=0)

    wcat2, wo2, wg2, wu2, wd2, gains2 = (
        both(wcat), both(w_out[0]), both(w_gate[0]), both(w_up[0]), both(w_down[0]),
        both(jnp.concatenate([attn_gain, mlp_gain], 0)),
    )

    own = jnp.stack([ctx, 2 * n_ctx - 1 - ctx])
    offs = jnp.arange(length, dtype=jnp.int32)
    pos = own[:, None] * length + offs[None, :]
    freq = ROPE_BASE ** (-(jnp.arange(0, HEAD_DIM, 2).astype(F32) / HEAD_DIM))
    phase_t = freq[None, :, None] * pos.astype(F32)[:, None, :]
    phase_t = jnp.concatenate([phase_t, phase_t], 1)
    cos_t, sin_t = jnp.cos(phase_t), jnp.sin(phase_t)

    def rows_of(t):
        t = jnp.swapaxes(t, 1, 2).reshape(2, n_t, sp, HEAD_DIM)
        return jnp.swapaxes(t, 0, 1).reshape(rows, HEAD_DIM)

    cos_r, sin_r = rows_of(cos_t), rows_of(sin_t)
    cos_n, sin_n = jnp.swapaxes(cos_t, 1, 2), jnp.swapaxes(sin_t, 1, 2)
    spread = np.zeros((HEAD_DIM, qkv_w), np.float32)
    turned_w = q_w + kv_w // 2
    spread[np.arange(turned_w) % HEAD_DIM, np.arange(turned_w)] = 1.0
    plain = np.where(np.arange(qkv_w) < turned_w, 0.0, 1.0).astype(np.float32)

    def wide_table(t):
        return lax.dot_general(
            t,
            jnp.asarray(spread),
            (((1,), (0,)), ((), ())),
            precision=lax.Precision.HIGHEST,
            preferred_element_type=F32,
        )

    cos_all, sin_all = wide_table(cos_r) + jnp.asarray(plain), wide_table(sin_r)

    def gain_of(layer, kind):
        return gains2[layer, kind : kind + 1]

    def attend(n1, layer, h=None):
        raw = nn(n1, wcat2[layer])
        qkv = (raw[:, :qkv_w] * cos_all + raw[:, qkv_w:] * sin_all).astype(BF)
        qkv = qkv.reshape(n_t, 2, sp, qkv_w)
        mix, mixt, lse, kv_all, *full = flash_forward(qkv, q_heads, h)
        mix = mix.reshape(rows, q_w)
        part = nn(mix, wo2[layer]).astype(BF)
        return part.reshape(n_t, 2, sp, d), (qkv, kv_all, mix, mixt, lse, *full)

    def feed(n2, layer):
        gate, up = nn(n2, wg2[layer]), nn(n2, wu2[layer])
        act = silu_product(gate, up).astype(BF)
        part = nn(act, wd2[layer]).astype(BF)
        return part.reshape(n_t, 2, sp, d), (gate, up, act)

    def feed_back(gm, layer, kept):
        gate, up, _ = kept
        dact = nt(gm, wd2[layer])
        _, pull = jax.vjp(silu_product, gate, up)
        dgate, dup = pull(dact)
        dgate, dup = dgate.astype(BF), dup.astype(BF)
        part = (nt(dgate, wg2[layer]) + nt(dup, wu2[layer])).astype(BF)
        return part.reshape(n_t, 2, sp, d), dgate, dup

    def attend_back(ga, layer, kept, *more):
        qkv, kv_all, _, mixt, lse = kept[:5]
        dmix = nt(ga, wo2[layer]).astype(BF).reshape(n_t, 2, sp, q_w)
        tables = (cos_t, sin_t, cos_n, sin_n)
        dqkv, *more = flash_backward(qkv, kv_all, dmix, mixt, lse, tables, *more)
        dqkv = dqkv.reshape(rows, qkv_w)
        part = nt(dqkv, wcat2[layer][:, :qkv_w]).astype(BF)
        return part.reshape(n_t, 2, sp, d), dqkv, more

    def exchange(*grads):
        out = []
        for g in grads:
            size = g.shape[0] // 2
            give = lax.dynamic_slice_in_dim(g, (1 - sec) * size, size, 0).astype(BF)
            keep = lax.dynamic_slice_in_dim(g, sec * size, size, 0)
            out.append((keep, swap(give)))
        return out

    def terms(halves):
        return [(keep + got.astype(F32)).astype(BF) for keep, got in halves]

    def cut(size, term):
        return term.reshape(2, -1, size, term.shape[1])

    def tie(x, others):
        return lax.optimization_barrier((x, others))

    flat = lambda v: v.reshape(rows, d)
    a0, a1, m0, m1 = gain_of(0, 0), gain_of(1, 0), gain_of(0, 1), gain_of(1, 1)

    h0 = x_own.astype(F32)
    n1_0 = flat(norm_gather(x_own, a0))
    part, att0 = attend(n1_0, 0)
    h2_0, full = sum_norm_gather(part, h0, m0, 0)
    n2_0 = flat(full)
    part, mlp0 = feed(n2_0, 0)
    h1, full = sum_norm_gather(part, h2_0, a1, 1)
    n1_1 = flat(full)
    part, att1 = attend(n1_1, 1, g_own)
    h2_1, full = sum_norm_gather(part, h1, m1, 2)
    n2_1 = flat(full)
    y_part, mlp1 = feed(n2_1, 1)

    gm1 = flat(att1[5])
    def backward(layer, gm, g, h, h2, n1, n2, att, mlp, kind, a_gain, m_gain, others, *more):
        part, dgate, dup = feed_back(gm, layer, mlp)
        wide = exchange(tn(n2, dgate), tn(n2, dup))
        down = exchange(tn(mlp[2], gm))
        zs = [cut(48, v) for v in terms(wide)]
        dh2, dm, wide, (full,) = back(part, h2, m_gain, g, 0, zs)
        ga = flat(full)
        out = exchange(tn(att[2], ga))
        part, dqkv, more = attend_back(ga, layer, att, *more)
        rest = terms(down + out + exchange(tn(n1, dqkv)))
        zs = [cut(size, v) for size, v in zip((32, 32, 64), rest)]
        if others is not None:
            others = jnp.concatenate([dm, *others], 0)
        dh, da, rest, full = back(part, h, a_gain, dh2, kind, zs, others)
        grads = [z.reshape(-1, z.shape[-1]) for z in (rest[0], *wide, *rest[1:])]
        return dh, full, (da, dm), grads, more

    g0, full, gains1, grads1, (y,) = backward(
        1, gm1, g_own.astype(F32), h1, h2_1, n1_1, n2_1, att1, mlp1, 1, a1, m1,
        None, y_part, h2_1,
    )
    dh0, _, (gains, _), grads0, _ = backward(
        0, flat(full[0]), g0.astype(F32), h0, h2_0, n1_0, n2_0, att0, mlp0, 2, a0, m0, gains1
    )
    gains = gains + swap(gains)
    gain_own = lax.dynamic_slice_in_dim(gains, 2 * sec, 2, 0)

    def to_owner(r0, r1):
        got0 = lax.ppermute(r0, "section", [(1, 0)])
        got1 = lax.ppermute(r1, "section", [(0, 1)])
        return jnp.where(
            first, jnp.concatenate([r0, got0], 0), jnp.concatenate([got1, r1], 0)
        ).astype(F32)

    gd, gg, gu, go, gqkv = (to_owner(a, b) for a, b in zip(grads0, grads1))
    half_kv = kv_w // 2
    return (
        from_own(y, BF),
        from_own(dh0, F32),
        gain_own[0:1],
        gqkv[None, :, :q_w],
        gqkv[None, :, q_w : q_w + half_kv],
        gqkv[None, :, q_w + half_kv :],
        go[None],
        gain_own[1:2],
        gg[None],
        gu[None],
        gd[None],
    )


def solution(mesh):
    rows = P(None, "ctx", None, "tensor", "section")
    gain = P("section", None)
    col = P("section", None, "tensor")
    row = P("section", "tensor", None)
    return jax.shard_map(
        on_device,
        mesh=mesh,
        in_specs=(rows, rows, P(), gain, col, col, col, row, gain, col, col, row),
        out_specs=(rows, rows, gain, col, col, col, row, gain, col, col, row),
        check_vma=False,
    )
```

```python
import functools

import jax
import jax.numpy as jnp
import numpy as np
from jax import lax
from jax.experimental import pallas as pl
from jax.experimental.pallas import tpu as pltpu
from jax.sharding import PartitionSpec as P

HEAD_DIM = 96
EPSILON = 1e-05
ROPE_BASE = 100000.0
LOG2E = 1.4426950408889634
BF = jnp.bfloat16
F32 = jnp.float32


def nn(a, b):
    return lax.dot_general(a, b, (((1,), (0,)), ((), ())), preferred_element_type=F32)


def nt(a, b):
    return lax.dot_general(a, b, (((1,), (1,)), ((), ())), preferred_element_type=F32)


def tn(a, b):
    return lax.dot_general(a, b, (((0,), (0,)), ((), ())), preferred_element_type=F32)


def head_of(x, h):
    return x[:, h * HEAD_DIM : (h + 1) * HEAD_DIM]


def transposed(x):
    return x.astype(F32).T.astype(BF)


def causal(length):
    keys = lax.broadcasted_iota(jnp.int32, (length, length), 0)
    queries = lax.broadcasted_iota(jnp.int32, (length, length), 1)
    return keys <= queries


def silu_product(gate, up):
    return gate * jax.nn.sigmoid(gate) * up


MESH = pl.DeviceIdType.MESH


def tensor_peers():
    t = lax.axis_index("tensor")
    return t, t + 1 - 2 * lax.rem(t, 2), lax.rem(t + 2, 4), 3 - t


def greet(tensor=True, line=False, after=False):
    barrier = pltpu.get_barrier_semaphore()
    count = 0
    if tensor:
        _, x, y, _ = tensor_peers()
        for peer in (x, y):
            pl.semaphore_signal(barrier, inc=1, device_id={"tensor": peer}, device_id_type=MESH)
        count += 2
    if line:
        c, _, has_left, has_right = ctx_ends()
        for there, peer in ((has_left, c - 1), (has_right, c + 1)):

            @pl.when(there)
            def _():
                pl.semaphore_signal(
                    barrier, inc=1, device_id={"ctx": peer}, device_id_type=MESH
                )

        count += has_left.astype(jnp.int32) + has_right.astype(jnp.int32)
    if after:
        count += lax.axis_index("section")
    pl.semaphore_wait(barrier, count)


def send(src, dst, sems, at, peer):
    return pltpu.make_async_remote_copy(
        src_ref=src,
        dst_ref=dst,
        send_sem=sems[0].at[at],
        recv_sem=sems[1].at[at],
        device_id={"tensor": peer},
        device_id_type=MESH,
    )


def gather_start(full, sems, chunks, q):
    t, x, y, _ = tensor_peers()
    j, at = chunks[q]
    near, far = (x, y) if j == 0 else (y, x)
    own = full.at[t, j, at]
    send(own, own, sems, (q, 0), near).start()
    send(own, own, sems, (q, 1), far).start()


def gather_pass(full, sems, chunks, q):
    _, x, y, _ = tensor_peers()
    j, at = chunks[q]
    near, far = (x, y) if j == 0 else (y, x)
    got = full.at[near, j, at]
    send(got, got, sems, (q, 0), near).wait_recv()
    send(got, got, sems, (q, 2), far).start()


def gather_end(full, sems, chunks, q):
    t, x, y, diag = tensor_peers()
    j, at = chunks[q]
    near, far = (x, y) if j == 0 else (y, x)
    for kind, owner in ((1, far), (2, diag)):
        got = full.at[owner, j, at]
        send(got, got, sems, (q, kind), far).wait_recv()


def gather_drain(full, sems, chunks, q):
    t, x, _, _ = tensor_peers()
    j, at = chunks[q]
    own = full.at[t, j, at]
    for kind in range(3):
        send(own, own, sems, (q, kind), x).wait_send()


def scatter_start(part, got, sems, chunks, q):
    _, x, y, diag = tensor_peers()
    j, at = chunks[q]
    far = y if j == 0 else x
    send(part.at[diag, j, at], got.at[0, j, at], sems, (q, 0), far).start()
    send(part.at[far, j, at], got.at[2, j, at], sems, (q, 2), far).start()


def scatter_pass(part, got, held, sems, chunks, q):
    _, x, y, _ = tensor_peers()
    j, at = chunks[q]
    near = x if j == 0 else y
    send(held.at[j, at], got.at[0, j, at], sems, (q, 0), near).wait_recv()
    held[j, at] = (part[near, j, at].astype(F32) + got[0, j, at].astype(F32)).astype(BF)
    send(held.at[j, at], got.at[1, j, at], sems, (q, 1), near).start()


def scatter_end(part, got, held, sems, chunks, q):
    t, x, _, _ = tensor_peers()
    j, at = chunks[q]
    for kind in (2, 1):
        send(held.at[j, at], got.at[kind, j, at], sems, (q, kind), x).wait_recv()
    return (
        part[t, j, at].astype(F32) + got[1, j, at].astype(F32) + got[2, j, at].astype(F32)
    )


def scatter_drain(part, got, sems, chunks, q):
    t, x, _, _ = tensor_peers()
    j, at = chunks[q]
    for kind in range(3):
        send(part.at[t, j, at], got.at[kind, j, at], sems, (q, kind), x).wait_send()


def inverse_rms(v):
    return lax.rsqrt(jnp.mean(v * v, axis=-1, keepdims=True) + EPSILON)


def norm_back(v, gain, dn):
    r = inverse_rms(v)
    unit = v * r
    scaled = dn * gain
    dv = r * (scaled - unit * jnp.mean(scaled * unit, axis=-1, keepdims=True))
    return dv, jnp.sum((dn * unit).reshape(-1, 8, v.shape[-1]), axis=0)


def chunk_list(sp):
    parts = 2
    size = sp // parts
    return [(j, pl.ds(s * size, size)) for s in range(parts) for j in range(2)]


def run_exchange(
    sp, part, finish, full, got, held, sc_sems, ga_sems,
    between=None, after=None, chain=None, turns=False,
):
    chunks = chunk_list(sp)
    n = range(len(chunks))
    greet(line=chain is not None, after=turns)
    steps = []
    if part is not None:
        for q in n:
            scatter_start(part, got, sc_sems, chunks, q)
        steps += [
            functools.partial(scatter_pass, part, got, held, sc_sems, chunks, q) for q in n
        ]

    def end(q):
        j, at = chunks[q]
        total = None if part is None else scatter_end(part, got, held, sc_sems, chunks, q)
        finish(j, at, total)
        if full is not None:
            gather_start(full, ga_sems, chunks, q)

    steps += [functools.partial(end, q) for q in n]
    if between is not None:
        steps.append(between)
    if full is not None:
        steps += [functools.partial(gather_pass, full, ga_sems, chunks, q) for q in n]
    if after is not None:
        steps.append(after)
    if full is not None:
        steps += [functools.partial(gather_end, full, ga_sems, chunks, q) for q in n]
    if chain is None:
        for step in steps:
            step()
    else:
        done = 0
        for time in range(chain.slots):
            chain.slot(time)
            goal = min(len(steps), int(len(steps) * (time + 1) / (0.8 * chain.slots)))
            for step in steps[done:goal]:
                step()
            done = goal
        for step in steps[done:]:
            step()
        chain.drain()
    if turns:

        @pl.when(lax.axis_index("section") == 0)
        def _():
            pl.semaphore_signal(
                pltpu.get_barrier_semaphore(),
                inc=1,
                device_id={"section": 1},
                device_id_type=MESH,
            )

    if full is not None:
        for q in n:
            gather_drain(full, ga_sems, chunks, q)
    if part is not None:
        for q in n:
            scatter_drain(part, got, sc_sems, chunks, q)


class Chain:
    def __init__(self, zs, gots, outs, sems):
        self.zs, self.gots, self.outs = zs, gots, outs
        self.sum_sems, self.back_sems = sems[:2], sems[2:]
        self.c, self.n, _, _ = ctx_ends()
        self.starts = [sum(z.shape[1] for z in zs[:k]) for k in range(len(zs))]
        self.hop = 2
        self.slots = sum(z.shape[1] for z in zs) + 2 * self.hop * (self.n - 1)

    def copy(self, src, dst, sems, d, k, i, peer):
        at = self.starts[k] + i
        return along(src[k].at[d, i], dst[k].at[d, i], sems[0].at[d, at], sems[1].at[d, at], peer)

    def sides(self, d):
        c, n = self.c, self.n
        return (c, c + 1, c - 1) if d == 0 else (n - 1 - c, c - 1, c + 1)

    def slot(self, time):
        n, zs, gots, outs = self.n, self.zs, self.gots, self.outs
        for d in range(2):
            place, ahead, behind = self.sides(d)
            due = time - self.hop * place
            due_back = time - self.hop * (2 * (n - 1) - place)
            for k in range(len(zs)):
                i = due - self.starts[k]
                going = (i >= 0) & (i < zs[k].shape[1])

                @pl.when(going & (place == 0))
                def _():
                    self.copy(zs, gots, self.sum_sems, d, k, i, ahead).start()

                @pl.when(going & (place > 0))
                def _():
                    self.copy(zs, gots, self.sum_sems, d, k, i, ahead).wait_recv()
                    total = (gots[k][d, i].astype(F32) + zs[k][d, i].astype(F32)).astype(BF)

                    @pl.when(place < n - 1)
                    def _():
                        gots[k][d, i] = total
                        self.copy(gots, gots, self.sum_sems, d, k, i, ahead).start()

                    @pl.when(place == n - 1)
                    def _():
                        outs[k][d, i] = total
                        self.copy(outs, outs, self.back_sems, d, k, i, behind).start()

                i_back = due_back - self.starts[k]
                coming = (i_back >= 0) & (i_back < zs[k].shape[1]) & (place < n - 1)

                @pl.when(coming)
                def _():
                    self.copy(outs, outs, self.back_sems, d, k, i_back, behind).wait_recv()

                    @pl.when(place > 0)
                    def _():
                        self.copy(outs, outs, self.back_sems, d, k, i_back, behind).start()

    def drain(self):
        for d in range(2):
            place, ahead, behind = self.sides(d)
            for k in range(len(self.zs)):

                def one(i, _):
                    @pl.when(place < self.n - 1)
                    def _():
                        self.copy(self.zs, self.gots, self.sum_sems, d, k, i, ahead).wait_send()

                    @pl.when(place > 0)
                    def _():
                        self.copy(
                            self.outs, self.outs, self.back_sems, d, k, i, behind
                        ).wait_send()

                    return 0

                lax.fori_loop(0, self.zs[k].shape[1], one, 0)


def chain_scratch(zs):
    sems = pltpu.SemaphoreType.DMA((2, sum(z.shape[1] for z in zs)))
    return [pltpu.VMEM(z.shape, BF) for z in zs] + [sems] * 4


def scatter_scratch(sp, d):
    n = len(chunk_list(sp))
    return [
        pltpu.VMEM((3, 2, sp, d), BF),
        pltpu.VMEM((2, sp, d), BF),
        pltpu.SemaphoreType.DMA((n, 3)),
        pltpu.SemaphoreType.DMA((n, 3)),
    ]


def gather_scratch(sp):
    n = len(chunk_list(sp))
    return [pltpu.SemaphoreType.DMA((n, 3)), pltpu.SemaphoreType.DMA((n, 3))]


def call(kernel, out_shape, scratch, ident, *operands):
    vm = pl.BlockSpec(memory_space=pltpu.VMEM)
    return pl.pallas_call(
        kernel,
        out_shape=out_shape,
        in_specs=[vm] * len(operands),
        out_specs=(vm,) * len(out_shape),
        scratch_shapes=scratch,
        compiler_params=pltpu.CompilerParams(
            collective_id=ident, has_side_effects=True, vmem_limit_bytes=50 * 2**20
        ),
    )(*operands)


def shapes_of(h):
    _, sp, d = h.shape
    return (
        jax.ShapeDtypeStruct((2, sp, d), F32),
        jax.ShapeDtypeStruct((4, 2, sp, d), BF),
        jax.ShapeDtypeStruct((1, d), F32),
        jax.ShapeDtypeStruct((2, sp, d), BF),
    )


def norm_gather_kernel(h, gain, full, *sems):
    t = lax.axis_index("tensor")

    def finish(j, at, _):
        v = h[j, at].astype(F32)
        full[t, j, at] = (v * inverse_rms(v) * gain[...]).astype(BF)

    run_exchange(h.shape[1], None, finish, full, None, None, None, sems, turns=True)


def norm_gather(h, gain):
    _, full, _, _ = shapes_of(h)
    return call(norm_gather_kernel, (full,), gather_scratch(h.shape[1]), 0, h, gain)[0]


def sum_norm_gather_kernel(kind, part, h, gain, total, full, got, held, s0, s1, g0, g1):
    t = lax.axis_index("tensor")

    def finish(j, at, term):
        v = h[j, at] + term
        if kind == 1:
            v = v.astype(BF).astype(F32)
        total[j, at] = v
        full[t, j, at] = (v * inverse_rms(v) * gain[...]).astype(BF)

    run_exchange(
        h.shape[1], part, finish, full, got, held, (s0, s1), (g0, g1), turns=kind == 0
    )


def sum_norm_gather(part, h, gain, kind):
    wide, full, _, _ = shapes_of(h)
    _, sp, d = h.shape
    return call(
        functools.partial(sum_norm_gather_kernel, kind),
        (wide, full),
        scatter_scratch(sp, d) + gather_scratch(sp),
        2 + kind,
        part, h, gain,
    )


def chain_kernel(count, *refs):
    zs, outs, gots = refs[:count], refs[count : 2 * count], refs[2 * count : 3 * count]
    chain = Chain(zs, gots, outs, refs[3 * count :])
    greet(tensor=False, line=True)
    for time in range(chain.slots):
        chain.slot(time)
    chain.drain()


def chain_sum(zs):
    return call(
        functools.partial(chain_kernel, len(zs)),
        tuple(jax.ShapeDtypeStruct(z.shape, BF) for z in zs),
        chain_scratch(zs),
        13,
        *zs,
    )


def line_sum(own, rows, sems):
    c, _, has_left, has_right = ctx_ends()
    sides = ((has_left, has_right, c + 1, 0), (has_right, has_left, c - 1, 1))
    for come, go, ahead, d in sides:
        copy = along(rows.at[2 * d + 1], rows.at[2 * d], sems[0].at[d], sems[1].at[d], ahead)
        rows[2 * d + 1] = own

        @pl.when(come)
        def _():
            copy.wait_recv()
            rows[2 * d + 1] = own + rows[2 * d]

        @pl.when(go)
        def _():
            copy.start()

    total = own
    for come, go, ahead, d in sides:
        copy = along(rows.at[2 * d + 1], rows.at[2 * d], sems[0].at[d], sems[1].at[d], ahead)
        total = total + jnp.where(come, rows[2 * d], 0.0)

        @pl.when(go)
        def _():
            copy.wait_send()

    return total


def back_kernel(kind, count, *refs):
    refs = list(refs)

    def take(size):
        out = refs[:size]
        del refs[:size]
        return out

    t, x, y, _ = tensor_peers()
    part, h, gain, g = take(4)
    others = take(1)[0] if kind == 2 else None
    zs = take(count)
    dv_out, dgain = take(2)
    z_out = take(count)
    full = take(1)[0] if kind != 2 else None
    got, held, s0, s1, rows, gs, gr = take(7)
    z_got = take(count)
    z_sems = take(4) if count else None
    ga = take(2) if kind != 2 else None
    line = take(3) if kind == 2 else None
    chain = Chain(zs, z_got, z_out, z_sems) if count else None
    rows[0] = jnp.zeros_like(rows[0])

    def finish(j, at, term):
        dv, dg = norm_back(h[j, at], gain[...], term)
        rows[0] = rows[0] + dg
        dv = dv + g[j, at].astype(F32)
        dv_out[j, at] = dv.astype(dv_out.dtype)
        if full is not None:
            full[t, j, at] = dv.astype(BF)

    def add_gains(step, peer):
        send(rows.at[2 * step], rows.at[2 * step + 1], (gs, gr), step, peer).start()

    def end_gains(step, peer):
        send(rows.at[2 * step], rows.at[2 * step + 1], (gs, gr), step, peer).wait()

    def between():
        add_gains(0, x)

    def after():
        end_gains(0, x)
        rows[2] = rows[0] + rows[1]
        add_gains(1, y)

    run_exchange(
        h.shape[1], part, finish, full, got, held, (s0, s1), ga, between, after, chain
    )
    end_gains(1, y)
    total = jnp.sum(rows[2] + rows[3], axis=0, keepdims=True)
    if kind == 2:
        blank = jnp.zeros((4, total.shape[1]), F32)
        total = jnp.concatenate([total, others[...], blank], axis=0)
        dgain[...] = line_sum(total, line[0], line[1:])
    else:
        dgain[...] = total


def back(part, h, gain, g, kind, ident, zs, others=None):
    wide, full, row, narrow = shapes_of(h)
    _, sp, d = h.shape
    row = jax.ShapeDtypeStruct((8, d), F32) if kind == 2 else row
    out = (narrow if kind == 1 else wide, row)
    out += tuple(jax.ShapeDtypeStruct(z.shape, BF) for z in zs)
    scratch = scatter_scratch(sp, d) + [
        pltpu.VMEM((4, 8, d), F32),
        pltpu.SemaphoreType.DMA((2,)),
        pltpu.SemaphoreType.DMA((2,)),
    ] + (chain_scratch(zs) if zs else [])
    if kind != 2:
        out += (full,)
        scratch += gather_scratch(sp)
    else:
        scratch += [
            pltpu.VMEM((4, 8, d), F32),
            pltpu.SemaphoreType.DMA((2,)),
            pltpu.SemaphoreType.DMA((2,)),
        ]
    operands = (part, h, gain, g) + (() if others is None else (others,)) + tuple(zs)
    res = call(
        functools.partial(back_kernel, kind, len(zs)), out, scratch, ident, *operands
    )
    return res[0], res[1], res[2 : 2 + len(zs)], res[2 + len(zs) :]


def ctx_ends():
    c = lax.axis_index("ctx")
    n = lax.axis_size("ctx")
    return c, n, c > 0, c < n - 1


def along(src, dst, send_sem, recv_sem, peer):
    return pltpu.make_async_remote_copy(
        src_ref=src,
        dst_ref=dst,
        send_sem=send_sem,
        recv_sem=recv_sem,
        device_id={"ctx": peer},
        device_id_type=MESH,
    )


def fwd_kernel(extra, *refs):
    if extra:
        (
            qkv_ref, h_ref, mix_ref, mixt_ref, lse_ref, kv_all, full,
            qt, m_s, l_s, acc, to_left, to_right, arrive, *ga,
        ) = refs
    else:
        (
            qkv_ref, mix_ref, mixt_ref, lse_ref, kv_all,
            qt, m_s, l_s, acc, to_left, to_right, arrive,
        ) = refs
    c, n, has_left, has_right = ctx_ends()
    n_t, _, sp, _ = qkv_ref.shape
    length, width = kv_all.shape[2:]
    kv_heads = width // (2 * HEAD_DIM)
    q_heads = qt.shape[1]
    q_w = q_heads * HEAD_DIM
    group = q_heads // kv_heads
    scale = HEAD_DIM**-0.5 * LOG2E

    def leftward(r, j):
        at = kv_all.at[r, j]
        return along(at, at, to_left.at[r, j], arrive.at[r, j], c - 1)

    def rightward(r):
        at = kv_all.at[r, 0]
        return along(at, at, to_right.at[r], arrive.at[r, 0], c + 1)

    def pass_left(r):
        @pl.when(has_left)
        def _():
            leftward(r, 0).start()
            leftward(r, 1).start()

    def pass_right(r):
        @pl.when(has_right)
        def _():
            rightward(r).start()

    for j in range(2):
        kv_all[c, j] = qkv_ref[:, j, :, q_w:].reshape(length, width)
    if extra:
        chunks = chunk_list(sp)
        t, _, _, _ = tensor_peers()

    greet(tensor=extra, line=True)
    pass_left(c)
    pass_right(c)
    if extra:
        for q in range(len(chunks)):
            j, at = chunks[q]
            full[t, j, at] = h_ref[j, at]
            gather_start(full, ga, chunks, q)

    for j in range(2):
        x = qkv_ref[:, j, :, :q_w].reshape(length, q_w)
        for h in range(q_heads):
            qt[j, h] = transposed(head_of(x, h))
    m_s[...] = jnp.full_like(m_s, -1e30)
    l_s[...] = jnp.zeros_like(l_s)
    acc[...] = jnp.zeros_like(acc)

    def pair(r, kj, j, masked):
        x = kv_all[r, kj]
        for h in range(q_heads):
            s = nn(head_of(x, h // group), qt[j, h]) * scale
            if masked:
                s = jnp.where(causal(length), s, -1e30)
            m_old = m_s[j, h]
            m_new = jnp.maximum(m_old, jnp.max(s, axis=0, keepdims=True))
            alpha = jnp.exp2(m_old - m_new)
            p = jnp.exp2(s - m_new)
            l_s[j, h] = l_s[j, h] * alpha + jnp.sum(p, axis=0, keepdims=True)
            m_s[j, h] = m_new
            value = transposed(head_of(x, kv_heads + h // group))
            acc[j, h] = acc[j, h] * alpha + nn(value, p.astype(BF))

    def diagonal(j, _):
        pair(c, j, j, True)
        return 0

    lax.fori_loop(0, 2, diagonal, 0)
    if extra:
        for q in range(len(chunks)):
            gather_pass(full, ga, chunks, q)

    def step(s, _):
        from_right = (s > 0) & (c + s < n)
        from_left = (s > 0) & (c - s >= 0)

        @pl.when(from_right)
        def _():
            leftward(c + s, 0).wait_recv()
            leftward(c + s, 1).wait_recv()
            pass_left(c + s)

        @pl.when(from_left)
        def _():
            rightward(c - s).wait_recv()
            pass_right(c - s)

        def item(i, _):
            side = i // 2
            k = lax.rem(i, 2)
            r = jnp.where(side == 0, c + s, c - s)
            ready = jnp.where(side == 0, from_right, from_left) | ((s == 0) & (i == 0))

            @pl.when(ready)
            def _():
                pair(r, jnp.where(side == 0, k, 0), jnp.where(side == 0, 1, k), False)

            return 0

        lax.fori_loop(0, 4, item, 0)
        return 0

    lax.fori_loop(0, n, step, 0)
    for j in range(2):
        outs = []
        for h in range(q_heads):
            out = acc[j, h] / l_s[j, h]
            mixt_ref[j, h] = out.astype(BF)
            lse_ref[j, h] = m_s[j, h] + jnp.log2(l_s[j, h])
            outs.append(out.T)
        mix_ref[:, j] = jnp.concatenate(outs, axis=-1).astype(BF).reshape(n_t, sp, -1)

    def drain(r, _):
        @pl.when((r >= c) & has_left)
        def _():
            leftward(r, 0).wait_send()
            leftward(r, 1).wait_send()

        @pl.when((r <= c) & has_right)
        def _():
            rightward(r).wait_send()

        return 0

    lax.fori_loop(0, n, drain, 0)
    if extra:
        for q in range(len(chunks)):
            gather_end(full, ga, chunks, q)
        for q in range(len(chunks)):
            gather_drain(full, ga, chunks, q)


def flash_forward(qkv, q_heads, h=None):
    n_t, _, sp, width = qkv.shape
    n = lax.axis_size("ctx")
    q_w = q_heads * HEAD_DIM
    length = n_t * sp
    rows = (2, q_heads, 1, length)
    cols = (2, q_heads, HEAD_DIM, length)
    extra = h is not None
    return call(
        functools.partial(fwd_kernel, extra),
        (
            jax.ShapeDtypeStruct((n_t, 2, sp, q_w), BF),
            jax.ShapeDtypeStruct(cols, BF),
            jax.ShapeDtypeStruct(rows, F32),
            jax.ShapeDtypeStruct((n, 2, length, width - q_w), BF),
        )
        + ((shapes_of(h)[1],) if extra else ()),
        [
            pltpu.VMEM(cols, BF),
            pltpu.VMEM(rows, F32),
            pltpu.VMEM(rows, F32),
            pltpu.VMEM(cols, F32),
            pltpu.SemaphoreType.DMA((n, 2)),
            pltpu.SemaphoreType.DMA((n,)),
            pltpu.SemaphoreType.DMA((n, 2)),
        ]
        + (gather_scratch(sp) if extra else []),
        9 if extra else 10,
        qkv,
        *((h,) if extra else ()),
    )


def bwd_kernel(extra, *refs):
    if extra:
        (
            qkv_ref, kv_all, do_ref, mixt_ref, lse_ref, cos_ref, sin_ref, cos_n, sin_n,
            part_ref, h_ref, out_ref, y_ref,
            qt, dot, qn, don, dl_s, dqt, acc, got_r, got_l, put_r, put_l, sr, ar, sl, al,
            sc_got, sc_held, *sc,
        ) = refs
    else:
        (
            qkv_ref, kv_all, do_ref, mixt_ref, lse_ref, cos_ref, sin_ref, cos_n, sin_n, out_ref,
            qt, dot, qn, don, dl_s, dqt, acc, got_r, got_l, put_r, put_l, sr, ar, sl, al,
        ) = refs
    c, n, has_left, has_right = ctx_ends()
    n_t, _, sp, _ = qkv_ref.shape
    length, width = kv_all.shape[2:]
    kv_heads = width // (2 * HEAD_DIM)
    q_heads = qt.shape[1]
    q_w = q_heads * HEAD_DIM
    group = q_heads // kv_heads
    scale = HEAD_DIM**-0.5
    half = HEAD_DIM // 2

    def rightward(r):
        return along(put_r.at[r], got_r.at[r], sr.at[r], ar.at[r], c + 1)

    def leftward(r):
        return along(put_l.at[r], got_l.at[r], sl.at[r], al.at[r], c - 1)

    greet(tensor=extra, line=True)
    if extra:
        chunks = chunk_list(sp)
        for q in range(len(chunks)):
            scatter_start(part_ref, sc_got, sc, chunks, q)
    for j in range(2):
        x = qkv_ref[:, j, :, :q_w].reshape(length, q_w)
        y = do_ref[:, j].reshape(length, q_w)
        for h in range(q_heads):
            a = head_of(x, h)
            qn[j, h] = a
            qt[j, h] = transposed(a)
            b = head_of(y, h)
            don[j, h] = b
            bt = b.astype(F32).T
            dot[j, h] = bt.astype(BF)
            dl_s[j, h] = jnp.sum(bt * mixt_ref[j, h].astype(F32), axis=0, keepdims=True)
    dqt[...] = jnp.zeros_like(dqt)

    def pair(r, kj, j, masked):
        x = kv_all[r, kj]
        for kh in range(kv_heads):
            key = head_of(x, kh)
            value = head_of(x, kv_heads + kh)
            key_t = transposed(key)
            dk = acc[kj, kh]
            dv = acc[kj, kv_heads + kh]
            for g in range(group):
                h = kh * group + g
                s = nn(key, qt[j, h]) * (scale * LOG2E)
                p = jnp.exp2(s - lse_ref[j, h])
                if masked:
                    p = jnp.where(causal(length), p, 0.0)
                dp = nn(value, dot[j, h])
                ds = (p * (dp - dl_s[j, h])).astype(BF)
                dv = dv + nn(p.astype(BF), don[j, h])
                dk = dk + nn(ds, qn[j, h])
                dqt[j, h] += nn(key_t, ds)
            acc[kj, kh] = dk
            acc[kj, kv_heads + kh] = dv

    def joined(kj):
        parts = [acc[kj, i] * (scale if i < kv_heads else 1.0) for i in range(2 * kv_heads)]
        return jnp.concatenate(parts, axis=-1)

    def finish_right(r, has_more):
        @pl.when(has_more)
        def _():
            rightward(r).wait_recv()
            for kj in range(2):
                put_r[r, kj] = (put_r[r, kj].astype(F32) + got_r[r, kj].astype(F32)).astype(BF)

        rightward(r).start()

    def finish_left(r, has_more):
        @pl.when(has_more)
        def _():
            leftward(r).wait_recv()
            put_l[r] = (put_l[r].astype(F32) + got_l[r].astype(F32)).astype(BF)

        leftward(r).start()

    def step(i, _):
        s = n - 1 - i

        def one_side(side, _):
            r = jnp.where(side == 0, c + s, c - s)
            ready = jnp.where(side == 0, c + s < n, (c - s >= 0) & (s > 0))

            @pl.when(ready)
            def _():
                acc[...] = jnp.zeros_like(acc)

                @pl.when(s == 0)
                def _():
                    def diagonal(j, _):
                        pair(c, j, j, True)
                        return 0

                    lax.fori_loop(0, 2, diagonal, 0)

                def item(k, _):
                    @pl.when((s > 0) | (k == 0))
                    def _():
                        pair(r, jnp.where(side == 0, k, 0), jnp.where(side == 0, 1, k), False)

                    return 0

                lax.fori_loop(0, 2, item, 0)

                @pl.when((side == 0) & (s > 0))
                def _():
                    for kj in range(2):
                        put_r[r, kj] = joined(kj).astype(BF)

                    @pl.when(jnp.logical_not(has_left))
                    def _():
                        rightward(r).start()

                @pl.when(side == 1)
                def _():
                    put_l[r] = joined(0).astype(BF)

                    @pl.when(jnp.logical_not(has_right))
                    def _():
                        leftward(r).start()

            return 0

        lax.fori_loop(0, 2, one_side, 0)
        late = s + 1

        @pl.when((c + late < n) & has_left)
        def _():
            finish_right(c + late, has_left)

        @pl.when((c - late >= 0) & has_right)
        def _():
            finish_left(c - late, has_right)

        return 0

    lax.fori_loop(0, 2, step, 0)
    if extra:
        for q in range(len(chunks)):
            scatter_pass(part_ref, sc_got, sc_held, sc, chunks, q)
    lax.fori_loop(2, n, step, 0)
    if extra:
        for q in range(len(chunks)):
            j, at = chunks[q]
            term = scatter_end(part_ref, sc_got, sc_held, sc, chunks, q)
            y_ref[j, at] = (h_ref[j, at] + term).astype(BF)
        for q in range(len(chunks)):
            scatter_drain(part_ref, sc_got, sc, chunks, q)
    for j in range(2):
        outs = []
        for h in range(q_heads):
            d = dqt[j, h] * scale
            sc = d * sin_ref[j]
            back = d * cos_ref[j] + jnp.concatenate([sc[half:], -sc[:half]], axis=0)
            outs.append(back.T)
        out_ref[:, j, :, :q_w] = jnp.concatenate(outs, axis=-1).astype(BF).reshape(n_t, sp, q_w)

    @pl.when(has_right)
    def _():
        leftward(c).wait_recv()

    @pl.when(has_left)
    def _():
        rightward(c).wait_recv()

    for kj in range(2):
        total = joined(kj)
        total += jnp.where(has_left, got_r[c, kj].astype(F32), 0.0)
        if kj == 0:
            total += jnp.where(has_right, got_l[c].astype(F32), 0.0)
        parts = []
        for kh in range(2 * kv_heads):
            d = head_of(total, kh)
            if kh < kv_heads:
                sc = d * sin_n[kj]
                d = d * cos_n[kj] + jnp.concatenate([sc[:, half:], -sc[:, :half]], axis=1)
            parts.append(d)
        out_ref[:, kj, :, q_w:] = jnp.concatenate(parts, axis=-1).astype(BF).reshape(n_t, sp, width)

    def drain(r, _):
        @pl.when((r > c) & has_right)
        def _():
            rightward(r).wait_send()

        @pl.when((r < c) & has_left)
        def _():
            leftward(r).wait_send()

        return 0

    lax.fori_loop(0, n, drain, 0)


def flash_backward(qkv, kv_all, do, mixt, lse, tables, part=None, h=None):
    n, _, length, width = kv_all.shape
    q_heads = mixt.shape[1]
    cols = pltpu.VMEM((2, q_heads, HEAD_DIM, length), BF)
    natural = pltpu.VMEM((2, q_heads, length, HEAD_DIM), BF)
    both = pltpu.VMEM((n, 2, length, width), BF)
    early = pltpu.VMEM((n, length, width), BF)
    sems = pltpu.SemaphoreType.DMA((n,))
    extra = part is not None
    return call(
        functools.partial(bwd_kernel, extra),
        (jax.ShapeDtypeStruct(qkv.shape, BF),) + ((shapes_of(h)[3],) if extra else ()),
        [
            cols,
            cols,
            natural,
            natural,
            pltpu.VMEM((2, q_heads, 1, length), F32),
            pltpu.VMEM((2, q_heads, HEAD_DIM, length), F32),
            pltpu.VMEM((2, width // HEAD_DIM, length, HEAD_DIM), F32),
            both,
            early,
            both,
            early,
            sems,
            sems,
            sems,
            sems,
        ]
        + (scatter_scratch(h.shape[1], h.shape[2]) if extra else []),
        12 if extra else 11,
        qkv, kv_all, do, mixt, lse, *tables, *((part, h) if extra else ()),
    )


def turn_matrix(heads, total):
    half = HEAD_DIM // 2
    m = np.zeros((total, total), np.float32)
    for h in range(heads):
        at = h * HEAD_DIM
        for i in range(half):
            m[at + half + i, at + i] = -1.0
            m[at + i, at + half + i] = 1.0
    return m


def swap(value):
    return lax.ppermute(value, "section", [(0, 1), (1, 0)])


def on_device(
    inputs, cotangent, block_order, attn_gain, w_query, key_weight, value_weight, w_out,
    mlp_gain, w_gate, w_up, w_down,
):
    sec = lax.axis_index("section")
    first = sec == 0
    ctx = lax.axis_index("ctx")
    n_t = lax.axis_size("tensor")
    n_ctx = lax.axis_size("ctx")
    _, _, _, sp, half_width = inputs.shape
    length = sp * n_t
    d = 2 * half_width
    rows = n_t * 2 * sp
    wq, wk, wv = w_query[0], key_weight[0], value_weight[0]
    q_w, kv_w = wq.shape[1], 2 * wk.shape[1]
    qkv_w = q_w + kv_w
    q_heads, kv_heads = q_w // HEAD_DIM, kv_w // (2 * HEAD_DIM)

    def to_own(x):
        keep = lax.dynamic_index_in_dim(x[:, 0], sec, 0, keepdims=False)
        give = lax.dynamic_index_in_dim(x[:, 0], 1 - sec, 0, keepdims=False)
        got = swap(give)
        return jnp.where(
            first, jnp.concatenate([keep, got], -1), jnp.concatenate([got, keep], -1)
        )

    def from_own(y, out_dtype):
        y = in_order(y)
        lo, hi = y[..., :half_width], y[..., half_width:]
        keep = jnp.where(first, lo, hi)
        got = swap(jnp.where(first, hi, lo).astype(BF)).astype(y.dtype)
        return jnp.where(first, jnp.stack([keep, got]), jnp.stack([got, keep]))[
            :, None
        ].astype(out_dtype)

    turned = lax.dynamic_index_in_dim(block_order, 2 * ctx, 0, keepdims=False) != ctx

    def in_order(x):
        return jnp.where(turned, jnp.stack([x[1], x[0]]), x)

    x_own = in_order(to_own(inputs))
    g_own = in_order(to_own(cotangent))

    turn_q = jnp.asarray(turn_matrix(q_heads, q_w), BF)
    turn_kv = turn_matrix(kv_heads, kv_w)
    wkv = jnp.concatenate([wk, wv], 1)
    wcat = jnp.concatenate(
        [wq, wkv, nn(wq, turn_q).astype(BF), nn(wkv, jnp.asarray(turn_kv, BF)).astype(BF)], 1
    )

    def both(w):
        return lax.all_gather(w, "section", axis=0)

    wcat2, wo2, wg2, wu2, wd2, gains2 = (
        both(wcat), both(w_out[0]), both(w_gate[0]), both(w_up[0]), both(w_down[0]),
        both(jnp.concatenate([attn_gain, mlp_gain], 0)),
    )

    own = jnp.stack([ctx, 2 * n_ctx - 1 - ctx])
    offs = jnp.arange(length, dtype=jnp.int32)
    pos = own[:, None] * length + offs[None, :]
    freq = ROPE_BASE ** (-(jnp.arange(0, HEAD_DIM, 2).astype(F32) / HEAD_DIM))
    phase_t = freq[None, :, None] * pos.astype(F32)[:, None, :]
    phase_t = jnp.concatenate([phase_t, phase_t], 1)
    cos_t, sin_t = jnp.cos(phase_t), jnp.sin(phase_t)

    def rows_of(t):
        t = jnp.swapaxes(t, 1, 2).reshape(2, n_t, sp, HEAD_DIM)
        return jnp.swapaxes(t, 0, 1).reshape(rows, HEAD_DIM)

    cos_r, sin_r = rows_of(cos_t), rows_of(sin_t)
    cos_n, sin_n = jnp.swapaxes(cos_t, 1, 2), jnp.swapaxes(sin_t, 1, 2)
    spread = np.zeros((HEAD_DIM, qkv_w), np.float32)
    turned_w = q_w + kv_w // 2
    spread[np.arange(turned_w) % HEAD_DIM, np.arange(turned_w)] = 1.0
    plain = np.where(np.arange(qkv_w) < turned_w, 0.0, 1.0).astype(np.float32)

    def wide_table(t):
        return lax.dot_general(
            t,
            jnp.asarray(spread),
            (((1,), (0,)), ((), ())),
            precision=lax.Precision.HIGHEST,
            preferred_element_type=F32,
        )

    cos_all, sin_all = wide_table(cos_r) + jnp.asarray(plain), wide_table(sin_r)

    def gain_of(layer, kind):
        return gains2[layer, kind : kind + 1]

    def attend(n1, layer, h=None):
        raw = nn(n1, wcat2[layer])
        qkv = (raw[:, :qkv_w] * cos_all + raw[:, qkv_w:] * sin_all).astype(BF)
        qkv = qkv.reshape(n_t, 2, sp, qkv_w)
        mix, mixt, lse, kv_all, *full = flash_forward(qkv, q_heads, h)
        mix = mix.reshape(rows, q_w)
        part = nn(mix, wo2[layer]).astype(BF)
        return part.reshape(n_t, 2, sp, d), (qkv, kv_all, mix, mixt, lse, *full)

    def feed(n2, layer):
        gate, up = nn(n2, wg2[layer]), nn(n2, wu2[layer])
        act = silu_product(gate, up).astype(BF)
        part = nn(act, wd2[layer]).astype(BF)
        return part.reshape(n_t, 2, sp, d), (gate, up, act)

    def feed_back(gm, layer, kept):
        gate, up, _ = kept
        dact = nt(gm, wd2[layer])
        _, pull = jax.vjp(silu_product, gate, up)
        dgate, dup = pull(dact)
        dgate, dup = dgate.astype(BF), dup.astype(BF)
        part = (nt(dgate, wg2[layer]) + nt(dup, wu2[layer])).astype(BF)
        return part.reshape(n_t, 2, sp, d), dgate, dup

    def attend_back(ga, layer, kept, *more):
        qkv, kv_all, _, mixt, lse = kept[:5]
        dmix = nt(ga, wo2[layer]).astype(BF).reshape(n_t, 2, sp, q_w)
        tables = (cos_t, sin_t, cos_n, sin_n)
        dqkv, *more = flash_backward(qkv, kv_all, dmix, mixt, lse, tables, *more)
        dqkv = dqkv.reshape(rows, qkv_w)
        part = nt(dqkv, wcat2[layer][:, :qkv_w]).astype(BF)
        return part.reshape(n_t, 2, sp, d), dqkv, more

    def halve(*grads):
        return [lax.psum_scatter(g, "section", scatter_dimension=0, tiled=True) for g in grads]

    def grad(left, right):
        return tn(left, right).astype(BF)

    def cut(size, term):
        return term.reshape(2, -1, size, term.shape[1])

    def tie(*values):
        return lax.optimization_barrier(values)

    flat = lambda v: v.reshape(rows, d)
    a0, a1, m0, m1 = gain_of(0, 0), gain_of(1, 0), gain_of(0, 1), gain_of(1, 1)

    h0 = x_own.astype(F32)
    n1_0 = flat(norm_gather(x_own, a0))
    part, att0 = attend(n1_0, 0)
    h2_0, full = sum_norm_gather(part, h0, m0, 0)
    n2_0 = flat(full)
    part, mlp0 = feed(n2_0, 0)
    h1, full = sum_norm_gather(part, h2_0, a1, 1)
    n1_1 = flat(full)
    part, att1 = attend(n1_1, 1, g_own)
    h2_1, full = sum_norm_gather(part, h1, m1, 2)
    n2_1 = flat(full)
    y_part, mlp1 = feed(n2_1, 1)

    gm1 = flat(att1[5])
    def joined(zs):
        return [z.reshape(-1, z.shape[-1]) for z in zs]

    part, dgate, dup = feed_back(gm1, 1, mlp1)
    raw = (grad(n2_1, dgate), grad(n2_1, dup), grad(mlp1[2], gm1))
    part, raw = tie(part, raw)
    wide1, down1 = halve(*raw[:2]), halve(raw[2])
    dh2_1, dm1, _, (full,) = back(part, h2_1, m1, g_own.astype(F32), 0, 5, ())
    ga = flat(full)
    part, dqkv, (y,) = attend_back(ga, 1, att1, y_part, h2_1)
    raw = (grad(att1[2], ga), grad(n1_1, dqkv))
    part, raw, wide1 = tie(part, raw, wide1)
    rest1 = down1 + halve(*raw)
    zs = [cut(48, v) for v in wide1]
    g0, da1, wide1, (full,) = back(part, h1, a1, dh2_1, 1, 6, zs)
    gm0 = flat(full)
    part, dgate, dup = feed_back(gm0, 0, mlp0)
    raw = (grad(n2_0, dgate), grad(n2_0, dup), grad(mlp0[2], gm0))
    part, raw, rest1 = tie(part, raw, rest1)
    wide0 = halve(*raw)
    zs = [cut(size, v) for size, v in zip((32, 32, 64), rest1)]
    dh2_0, dm0, rest1, (full,) = back(part, h2_0, m0, g0.astype(F32), 0, 7, zs)
    ga = flat(full)
    part, dqkv, _ = attend_back(ga, 0, att0)
    raw = (grad(att0[2], ga), grad(n1_0, dqkv))
    part, raw, wide0 = tie(part, raw, wide0)
    rest0 = halve(*raw)
    zs = [cut(size, v) for size, v in zip((48, 48, 32), wide0)]
    others = jnp.concatenate([dm0, da1, dm1], 0)
    dh0, gains, wide0, _ = back(part, h0, a0, dh2_0, 2, 8, zs, others)
    rest0, dh0, gains = tie(rest0, dh0, gains)
    rest0 = chain_sum([cut(size, v) for size, v in zip((32, 64), rest0)])
    wide1, rest1, wide0, rest0 = joined(wide1), joined(rest1), joined(wide0), joined(rest0)
    y, dh0, gains, wide1, rest1, wide0, rest0 = tie(y, dh0, gains, wide1, rest1, wide0, rest0)
    grads1 = (rest1[0], *wide1, *rest1[1:])
    grads0 = (wide0[2], *wide0[:2], *rest0)
    gains = gains + swap(gains)
    gain_own = lax.dynamic_slice_in_dim(gains, 2 * sec, 2, 0)

    def to_owner(r0, r1):
        got = swap(jnp.where(first, r1, r0))
        keep = jnp.where(first, r0, r1)
        return jnp.where(
            first, jnp.concatenate([keep, got], 0), jnp.concatenate([got, keep], 0)
        ).astype(F32)

    gd, gg, gu, go, gqkv = (to_owner(a, b) for a, b in zip(grads0, grads1))
    half_kv = kv_w // 2
    return (
        from_own(y, BF),
        from_own(dh0, F32),
        gain_own[0:1],
        gqkv[None, :, :q_w],
        gqkv[None, :, q_w : q_w + half_kv],
        gqkv[None, :, q_w + half_kv :],
        go[None],
        gain_own[1:2],
        gg[None],
        gu[None],
        gd[None],
    )


def solution(mesh):
    rows = P(None, "ctx", None, "tensor", "section")
    gain = P("section", None)
    col = P("section", None, "tensor")
    row = P("section", "tensor", None)
    return jax.shard_map(
        on_device,
        mesh=mesh,
        in_specs=(rows, rows, P(), gain, col, col, col, row, gain, col, col, row),
        out_specs=(rows, rows, gain, col, col, col, row, gain, col, col, row),
        check_vma=False,
    )
```

```python
import functools

import jax
import jax.numpy as jnp
import numpy as np
from jax import lax
from jax.experimental import pallas as pl
from jax.experimental.pallas import tpu as pltpu
from jax.sharding import PartitionSpec as P

HEAD_DIM = 96
EPSILON = 1e-05
ROPE_BASE = 100000.0
LOG2E = 1.4426950408889634
BF = jnp.bfloat16
F32 = jnp.float32


def nn(a, b):
    return lax.dot_general(a, b, (((1,), (0,)), ((), ())), preferred_element_type=F32)


def nt(a, b):
    return lax.dot_general(a, b, (((1,), (1,)), ((), ())), preferred_element_type=F32)


def tn(a, b):
    return lax.dot_general(a, b, (((0,), (0,)), ((), ())), preferred_element_type=F32)


def head_of(x, h):
    return x[:, h * HEAD_DIM : (h + 1) * HEAD_DIM]


def transposed(x):
    return x.astype(F32).T.astype(BF)


def causal(length):
    keys = lax.broadcasted_iota(jnp.int32, (length, length), 0)
    queries = lax.broadcasted_iota(jnp.int32, (length, length), 1)
    return keys <= queries


MESH = pl.DeviceIdType.MESH


def tensor_peers():
    t = lax.axis_index("tensor")
    return t, t + 1 - 2 * lax.rem(t, 2), lax.rem(t + 2, 4), 3 - t


def greet(tensor=True, line=False, after=False):
    barrier = pltpu.get_barrier_semaphore()
    count = 0
    if tensor:
        _, x, y, _ = tensor_peers()
        for peer in (x, y):
            pl.semaphore_signal(barrier, inc=1, device_id={"tensor": peer}, device_id_type=MESH)
        count += 2
    if line:
        c, _, has_left, has_right = ctx_ends()
        for there, peer in ((has_left, c - 1), (has_right, c + 1)):

            @pl.when(there)
            def _():
                pl.semaphore_signal(
                    barrier, inc=1, device_id={"ctx": peer}, device_id_type=MESH
                )

        count += has_left.astype(jnp.int32) + has_right.astype(jnp.int32)
    if after:
        count += lax.axis_index("section")
    pl.semaphore_wait(barrier, count)


def send(src, dst, sems, at, peer):
    return pltpu.make_async_remote_copy(
        src_ref=src,
        dst_ref=dst,
        send_sem=sems[0].at[at],
        recv_sem=sems[1].at[at],
        device_id={"tensor": peer},
        device_id_type=MESH,
    )


def gather_start(full, sems, chunks, q):
    t, x, y, _ = tensor_peers()
    j, at = chunks[q]
    near, far = (x, y) if j == 0 else (y, x)
    own = full.at[t, j, at]
    send(own, own, sems, (q, 0), near).start()
    send(own, own, sems, (q, 1), far).start()


def gather_pass(full, sems, chunks, q):
    _, x, y, _ = tensor_peers()
    j, at = chunks[q]
    near, far = (x, y) if j == 0 else (y, x)
    got = full.at[near, j, at]
    send(got, got, sems, (q, 0), near).wait_recv()
    send(got, got, sems, (q, 2), far).start()


def gather_end(full, sems, chunks, q):
    t, x, y, diag = tensor_peers()
    j, at = chunks[q]
    near, far = (x, y) if j == 0 else (y, x)
    for kind, owner in ((1, far), (2, diag)):
        got = full.at[owner, j, at]
        send(got, got, sems, (q, kind), far).wait_recv()


def gather_drain(full, sems, chunks, q):
    t, x, _, _ = tensor_peers()
    j, at = chunks[q]
    own = full.at[t, j, at]
    for kind in range(3):
        send(own, own, sems, (q, kind), x).wait_send()


def scatter_start(part, got, sems, chunks, q):
    _, x, y, diag = tensor_peers()
    j, at = chunks[q]
    far = y if j == 0 else x
    send(part.at[diag, j, at], got.at[0, j, at], sems, (q, 0), far).start()
    send(part.at[far, j, at], got.at[2, j, at], sems, (q, 2), far).start()


def scatter_pass(part, got, held, sems, chunks, q):
    _, x, y, _ = tensor_peers()
    j, at = chunks[q]
    near = x if j == 0 else y
    send(held.at[j, at], got.at[0, j, at], sems, (q, 0), near).wait_recv()
    held[j, at] = (part[near, j, at].astype(F32) + got[0, j, at].astype(F32)).astype(BF)
    send(held.at[j, at], got.at[1, j, at], sems, (q, 1), near).start()


def scatter_end(part, got, held, sems, chunks, q):
    t, x, _, _ = tensor_peers()
    j, at = chunks[q]
    for kind in (2, 1):
        send(held.at[j, at], got.at[kind, j, at], sems, (q, kind), x).wait_recv()
    return (
        part[t, j, at].astype(F32) + got[1, j, at].astype(F32) + got[2, j, at].astype(F32)
    )


def scatter_drain(part, got, sems, chunks, q):
    t, x, _, _ = tensor_peers()
    j, at = chunks[q]
    for kind in range(3):
        send(part.at[t, j, at], got.at[kind, j, at], sems, (q, kind), x).wait_send()


def inverse_rms(v):
    return lax.rsqrt(jnp.mean(v * v, axis=-1, keepdims=True) + EPSILON)


def norm_back(v, gain, dn):
    r = inverse_rms(v)
    unit = v * r
    scaled = dn * gain
    dv = r * (scaled - unit * jnp.mean(scaled * unit, axis=-1, keepdims=True))
    return dv, jnp.sum((dn * unit).reshape(-1, 8, v.shape[-1]), axis=0)


def chunk_list(sp):
    parts = 2
    size = sp // parts
    return [(j, pl.ds(s * size, size)) for s in range(parts) for j in range(2)]


def run_exchange(
    sp, part, finish, full, got, held, sc_sems, ga_sems,
    between=None, after=None, chain=None, turns=False,
):
    chunks = chunk_list(sp)
    n = range(len(chunks))
    greet(line=chain is not None, after=turns)
    steps = []
    if part is not None:
        for q in n:
            scatter_start(part, got, sc_sems, chunks, q)
        steps += [
            functools.partial(scatter_pass, part, got, held, sc_sems, chunks, q) for q in n
        ]

    def end(q):
        j, at = chunks[q]
        total = None if part is None else scatter_end(part, got, held, sc_sems, chunks, q)
        finish(j, at, total)
        if full is not None:
            gather_start(full, ga_sems, chunks, q)

    steps += [functools.partial(end, q) for q in n]
    if between is not None:
        steps.append(between)
    if full is not None:
        steps += [functools.partial(gather_pass, full, ga_sems, chunks, q) for q in n]
    if after is not None:
        steps.append(after)
    if full is not None:
        steps += [functools.partial(gather_end, full, ga_sems, chunks, q) for q in n]
    if chain is None:
        for step in steps:
            step()
    else:
        done = 0
        for time in range(chain.slots):
            chain.slot(time)
            goal = min(len(steps), int(len(steps) * (time + 1) / (0.8 * chain.slots)))
            for step in steps[done:goal]:
                step()
            done = goal
        for step in steps[done:]:
            step()
        chain.drain()
    if turns:

        @pl.when(lax.axis_index("section") == 0)
        def _():
            pl.semaphore_signal(
                pltpu.get_barrier_semaphore(),
                inc=1,
                device_id={"section": 1},
                device_id_type=MESH,
            )

    if full is not None:
        for q in n:
            gather_drain(full, ga_sems, chunks, q)
    if part is not None:
        for q in n:
            scatter_drain(part, got, sc_sems, chunks, q)


class Chain:
    def __init__(self, zs, gots, outs, sems):
        self.zs, self.gots, self.outs = zs, gots, outs
        self.sum_sems, self.back_sems = sems[:2], sems[2:]
        self.c, self.n, _, _ = ctx_ends()
        self.starts = [sum(z.shape[1] for z in zs[:k]) for k in range(len(zs))]
        self.hop = 2
        self.slots = sum(z.shape[1] for z in zs) + 2 * self.hop * (self.n - 1)

    def copy(self, src, dst, sems, d, k, i, peer):
        at = self.starts[k] + i
        return along(src[k].at[d, i], dst[k].at[d, i], sems[0].at[d, at], sems[1].at[d, at], peer)

    def sides(self, d):
        c, n = self.c, self.n
        return (c, c + 1, c - 1) if d == 0 else (n - 1 - c, c - 1, c + 1)

    def slot(self, time):
        n, zs, gots, outs = self.n, self.zs, self.gots, self.outs
        for d in range(2):
            place, ahead, behind = self.sides(d)
            due = time - self.hop * place
            due_back = time - self.hop * (2 * (n - 1) - place)
            for k in range(len(zs)):
                i = due - self.starts[k]
                going = (i >= 0) & (i < zs[k].shape[1])

                @pl.when(going & (place == 0))
                def _():
                    self.copy(zs, gots, self.sum_sems, d, k, i, ahead).start()

                @pl.when(going & (place > 0))
                def _():
                    self.copy(zs, gots, self.sum_sems, d, k, i, ahead).wait_recv()
                    total = (gots[k][d, i].astype(F32) + zs[k][d, i].astype(F32)).astype(BF)

                    @pl.when(place < n - 1)
                    def _():
                        gots[k][d, i] = total
                        self.copy(gots, gots, self.sum_sems, d, k, i, ahead).start()

                    @pl.when(place == n - 1)
                    def _():
                        outs[k][d, i] = total
                        self.copy(outs, outs, self.back_sems, d, k, i, behind).start()

                i_back = due_back - self.starts[k]
                coming = (i_back >= 0) & (i_back < zs[k].shape[1]) & (place < n - 1)

                @pl.when(coming)
                def _():
                    self.copy(outs, outs, self.back_sems, d, k, i_back, behind).wait_recv()

                    @pl.when(place > 0)
                    def _():
                        self.copy(outs, outs, self.back_sems, d, k, i_back, behind).start()

    def drain(self):
        for d in range(2):
            place, ahead, behind = self.sides(d)
            for k in range(len(self.zs)):

                def one(i, _):
                    @pl.when(place < self.n - 1)
                    def _():
                        self.copy(self.zs, self.gots, self.sum_sems, d, k, i, ahead).wait_send()

                    @pl.when(place > 0)
                    def _():
                        self.copy(
                            self.outs, self.outs, self.back_sems, d, k, i, behind
                        ).wait_send()

                    return 0

                lax.fori_loop(0, self.zs[k].shape[1], one, 0)


def chain_scratch(zs):
    sems = pltpu.SemaphoreType.DMA((2, sum(z.shape[1] for z in zs)))
    return [pltpu.VMEM(z.shape, BF) for z in zs] + [sems] * 4


def scatter_scratch(sp, d):
    n = len(chunk_list(sp))
    return [
        pltpu.VMEM((3, 2, sp, d), BF),
        pltpu.VMEM((2, sp, d), BF),
        pltpu.SemaphoreType.DMA((n, 3)),
        pltpu.SemaphoreType.DMA((n, 3)),
    ]


def gather_scratch(sp):
    n = len(chunk_list(sp))
    return [pltpu.SemaphoreType.DMA((n, 3)), pltpu.SemaphoreType.DMA((n, 3))]


def size_in_vmem(shape, dtype):
    if len(shape) < 2:
        return 4096
    lanes = -(-shape[-1] // 128) * 128
    rows = -(-shape[-2] // 16) * 16
    return int(np.prod(shape[:-2])) * rows * lanes * jnp.dtype(dtype).itemsize


def call(kernel, out_shape, scratch, ident, *operands, spare=10):
    vm = pl.BlockSpec(memory_space=pltpu.VMEM)
    held = list(operands) + list(out_shape) + [v for v in scratch if hasattr(v, "memory_space")]
    total = sum(size_in_vmem(v.shape, v.dtype) for v in held if v.dtype in (BF, F32))
    limit = min(50 * 2**20, total + spare * 2**20)
    return pl.pallas_call(
        kernel,
        out_shape=out_shape,
        in_specs=[vm] * len(operands),
        out_specs=(vm,) * len(out_shape),
        scratch_shapes=scratch,
        compiler_params=pltpu.CompilerParams(
            collective_id=ident, has_side_effects=True, vmem_limit_bytes=limit
        ),
    )(*operands)


def shapes_of(h):
    _, sp, d = h.shape
    return (
        jax.ShapeDtypeStruct((2, sp, d), F32),
        jax.ShapeDtypeStruct((4, 2, sp, d), BF),
        jax.ShapeDtypeStruct((1, d), F32),
        jax.ShapeDtypeStruct((2, sp, d), BF),
    )


def norm_gather_kernel(h, gain, full, *sems):
    t = lax.axis_index("tensor")

    def finish(j, at, _):
        v = h[j, at].astype(F32)
        full[t, j, at] = (v * inverse_rms(v) * gain[...]).astype(BF)

    run_exchange(h.shape[1], None, finish, full, None, None, None, sems, turns=True)


def norm_gather(h, gain):
    _, full, _, _ = shapes_of(h)
    return call(norm_gather_kernel, (full,), gather_scratch(h.shape[1]), 0, h, gain)[0]


def sum_norm_gather_kernel(kind, part, h, gain, total, full, got, held, s0, s1, g0, g1):
    t = lax.axis_index("tensor")

    def finish(j, at, term):
        v = h[j, at] + term
        if kind == 1:
            v = v.astype(BF).astype(F32)
        total[j, at] = v
        full[t, j, at] = (v * inverse_rms(v) * gain[...]).astype(BF)

    run_exchange(
        h.shape[1], part, finish, full, got, held, (s0, s1), (g0, g1), turns=kind == 0
    )


def sum_norm_gather(part, h, gain, kind):
    wide, full, _, _ = shapes_of(h)
    _, sp, d = h.shape
    return call(
        functools.partial(sum_norm_gather_kernel, kind),
        (wide, full),
        scatter_scratch(sp, d) + gather_scratch(sp),
        2 + kind,
        part, h, gain,
    )


def chain_kernel(count, *refs):
    zs, outs, gots = refs[:count], refs[count : 2 * count], refs[2 * count : 3 * count]
    chain = Chain(zs, gots, outs, refs[3 * count :])
    greet(tensor=False, line=True)
    for time in range(chain.slots):
        chain.slot(time)
    chain.drain()


def chain_sum(zs):
    return call(
        functools.partial(chain_kernel, len(zs)),
        tuple(jax.ShapeDtypeStruct(z.shape, BF) for z in zs),
        chain_scratch(zs),
        13,
        *zs,
    )


def line_sum(own, rows, sems):
    c, _, has_left, has_right = ctx_ends()
    sides = ((has_left, has_right, c + 1, 0), (has_right, has_left, c - 1, 1))
    for come, go, ahead, d in sides:
        copy = along(rows.at[2 * d + 1], rows.at[2 * d], sems[0].at[d], sems[1].at[d], ahead)
        rows[2 * d + 1] = own

        @pl.when(come)
        def _():
            copy.wait_recv()
            rows[2 * d + 1] = own + rows[2 * d]

        @pl.when(go)
        def _():
            copy.start()

    total = own
    for come, go, ahead, d in sides:
        copy = along(rows.at[2 * d + 1], rows.at[2 * d], sems[0].at[d], sems[1].at[d], ahead)
        total = total + jnp.where(come, rows[2 * d], 0.0)

        @pl.when(go)
        def _():
            copy.wait_send()

    return total


def back_kernel(kind, count, *refs):
    refs = list(refs)

    def take(size):
        out = refs[:size]
        del refs[:size]
        return out

    t, x, y, _ = tensor_peers()
    part, h, gain, g = take(4)
    others = take(1)[0] if kind == 2 else None
    zs = take(count)
    dv_out, dgain = take(2)
    z_out = take(count)
    full = take(1)[0] if kind != 2 else None
    got, held, s0, s1, rows, gs, gr = take(7)
    z_got = take(count)
    z_sems = take(4) if count else None
    ga = take(2) if kind != 2 else None
    line = take(3) if kind == 2 else None
    chain = Chain(zs, z_got, z_out, z_sems) if count else None
    rows[0] = jnp.zeros_like(rows[0])

    def finish(j, at, term):
        dv, dg = norm_back(h[j, at], gain[...], term)
        rows[0] = rows[0] + dg
        dv = dv + g[j, at].astype(F32)
        dv_out[j, at] = dv.astype(dv_out.dtype)
        if full is not None:
            full[t, j, at] = dv.astype(BF)

    def add_gains(step, peer):
        send(rows.at[2 * step], rows.at[2 * step + 1], (gs, gr), step, peer).start()

    def end_gains(step, peer):
        send(rows.at[2 * step], rows.at[2 * step + 1], (gs, gr), step, peer).wait()

    def between():
        add_gains(0, x)

    def after():
        end_gains(0, x)
        rows[2] = rows[0] + rows[1]
        add_gains(1, y)

    run_exchange(
        h.shape[1], part, finish, full, got, held, (s0, s1), ga, between, after, chain
    )
    end_gains(1, y)
    total = jnp.sum(rows[2] + rows[3], axis=0, keepdims=True)
    if kind == 2:
        blank = jnp.zeros((4, total.shape[1]), F32)
        total = jnp.concatenate([total, others[...], blank], axis=0)
        dgain[...] = line_sum(total, line[0], line[1:])
    else:
        dgain[...] = total


def back(part, h, gain, g, kind, ident, zs, others=None):
    wide, full, row, narrow = shapes_of(h)
    _, sp, d = h.shape
    row = jax.ShapeDtypeStruct((8, d), F32) if kind == 2 else row
    out = (narrow if kind == 1 else wide, row)
    out += tuple(jax.ShapeDtypeStruct(z.shape, BF) for z in zs)
    scratch = scatter_scratch(sp, d) + [
        pltpu.VMEM((4, 8, d), F32),
        pltpu.SemaphoreType.DMA((2,)),
        pltpu.SemaphoreType.DMA((2,)),
    ] + (chain_scratch(zs) if zs else [])
    if kind != 2:
        out += (full,)
        scratch += gather_scratch(sp)
    else:
        scratch += [
            pltpu.VMEM((4, 8, d), F32),
            pltpu.SemaphoreType.DMA((2,)),
            pltpu.SemaphoreType.DMA((2,)),
        ]
    operands = (part, h, gain, g) + (() if others is None else (others,)) + tuple(zs)
    res = call(
        functools.partial(back_kernel, kind, len(zs)), out, scratch, ident, *operands, spare=50
    )
    return res[0], res[1], res[2 : 2 + len(zs)], res[2 + len(zs) :]


def ctx_ends():
    c = lax.axis_index("ctx")
    n = lax.axis_size("ctx")
    return c, n, c > 0, c < n - 1


def along(src, dst, send_sem, recv_sem, peer):
    return pltpu.make_async_remote_copy(
        src_ref=src,
        dst_ref=dst,
        send_sem=send_sem,
        recv_sem=recv_sem,
        device_id={"ctx": peer},
        device_id_type=MESH,
    )


def fwd_kernel(extra, *refs):
    if extra:
        (
            qkv_ref, h_ref, mix_ref, mixt_ref, lse_ref, kv_all, full,
            qt, m_s, l_s, acc, to_left, to_right, arrive, *ga,
        ) = refs
    else:
        (
            qkv_ref, mix_ref, mixt_ref, lse_ref, kv_all,
            qt, m_s, l_s, acc, to_left, to_right, arrive,
        ) = refs
    c, n, has_left, has_right = ctx_ends()
    n_t, _, sp, _ = qkv_ref.shape
    length, width = kv_all.shape[2:]
    kv_heads = width // (2 * HEAD_DIM)
    q_heads = qt.shape[1]
    q_w = q_heads * HEAD_DIM
    group = q_heads // kv_heads
    scale = HEAD_DIM**-0.5 * LOG2E

    def leftward(r, j):
        at = kv_all.at[r, j]
        return along(at, at, to_left.at[r, j], arrive.at[r, j], c - 1)

    def rightward(r):
        at = kv_all.at[r, 0]
        return along(at, at, to_right.at[r], arrive.at[r, 0], c + 1)

    def pass_left(r):
        @pl.when(has_left)
        def _():
            leftward(r, 0).start()
            leftward(r, 1).start()

    def pass_right(r):
        @pl.when(has_right)
        def _():
            rightward(r).start()

    for j in range(2):
        kv_all[c, j] = qkv_ref[:, j, :, q_w:].reshape(length, width)
    if extra:
        chunks = chunk_list(sp)
        t, _, _, _ = tensor_peers()

    greet(tensor=extra, line=True)
    pass_left(c)
    pass_right(c)
    if extra:
        for q in range(len(chunks)):
            j, at = chunks[q]
            full[t, j, at] = h_ref[j, at]
            gather_start(full, ga, chunks, q)

    for j in range(2):
        x = qkv_ref[:, j, :, :q_w].reshape(length, q_w)
        for h in range(q_heads):
            qt[j, h] = transposed(head_of(x, h))
    m_s[...] = jnp.full_like(m_s, -1e30)
    l_s[...] = jnp.zeros_like(l_s)
    acc[...] = jnp.zeros_like(acc)

    def pair(r, kj, j, masked):
        x = kv_all[r, kj]
        for h in range(q_heads):
            s = nn(head_of(x, h // group), qt[j, h]) * scale
            if masked:
                s = jnp.where(causal(length), s, -1e30)
            m_old = m_s[j, h]
            m_new = jnp.maximum(m_old, jnp.max(s, axis=0, keepdims=True))
            alpha = jnp.exp2(m_old - m_new)
            p = jnp.exp2(s - m_new)
            l_s[j, h] = l_s[j, h] * alpha + jnp.sum(p, axis=0, keepdims=True)
            m_s[j, h] = m_new
            value = transposed(head_of(x, kv_heads + h // group))
            acc[j, h] = acc[j, h] * alpha + nn(value, p.astype(BF))

    def diagonal(j, _):
        pair(c, j, j, True)
        return 0

    lax.fori_loop(0, 2, diagonal, 0)
    if extra:
        for q in range(len(chunks)):
            gather_pass(full, ga, chunks, q)

    def step(s, _):
        from_right = (s > 0) & (c + s < n)
        from_left = (s > 0) & (c - s >= 0)

        @pl.when(from_right)
        def _():
            leftward(c + s, 0).wait_recv()
            leftward(c + s, 1).wait_recv()
            pass_left(c + s)

        @pl.when(from_left)
        def _():
            rightward(c - s).wait_recv()
            pass_right(c - s)

        def item(i, _):
            side = i // 2
            k = lax.rem(i, 2)
            r = jnp.where(side == 0, c + s, c - s)
            ready = jnp.where(side == 0, from_right, from_left) | ((s == 0) & (i == 0))

            @pl.when(ready)
            def _():
                pair(r, jnp.where(side == 0, k, 0), jnp.where(side == 0, 1, k), False)

            return 0

        lax.fori_loop(0, 4, item, 0)
        return 0

    lax.fori_loop(0, n, step, 0)
    for j in range(2):
        outs = []
        for h in range(q_heads):
            out = acc[j, h] / l_s[j, h]
            mixt_ref[j, h] = out.astype(BF)
            lse_ref[j, h] = m_s[j, h] + jnp.log2(l_s[j, h])
            outs.append(out.T)
        mix_ref[:, j] = jnp.concatenate(outs, axis=-1).astype(BF).reshape(n_t, sp, -1)

    def drain(r, _):
        @pl.when((r >= c) & has_left)
        def _():
            leftward(r, 0).wait_send()
            leftward(r, 1).wait_send()

        @pl.when((r <= c) & has_right)
        def _():
            rightward(r).wait_send()

        return 0

    lax.fori_loop(0, n, drain, 0)
    if extra:
        for q in range(len(chunks)):
            gather_end(full, ga, chunks, q)
        for q in range(len(chunks)):
            gather_drain(full, ga, chunks, q)


def flash_forward(qkv, q_heads, h=None):
    n_t, _, sp, width = qkv.shape
    n = lax.axis_size("ctx")
    q_w = q_heads * HEAD_DIM
    length = n_t * sp
    rows = (2, q_heads, 1, length)
    cols = (2, q_heads, HEAD_DIM, length)
    extra = h is not None
    return call(
        functools.partial(fwd_kernel, extra),
        (
            jax.ShapeDtypeStruct((n_t, 2, sp, q_w), BF),
            jax.ShapeDtypeStruct(cols, BF),
            jax.ShapeDtypeStruct(rows, F32),
            jax.ShapeDtypeStruct((n, 2, length, width - q_w), BF),
        )
        + ((shapes_of(h)[1],) if extra else ()),
        [
            pltpu.VMEM(cols, BF),
            pltpu.VMEM(rows, F32),
            pltpu.VMEM(rows, F32),
            pltpu.VMEM(cols, F32),
            pltpu.SemaphoreType.DMA((n, 2)),
            pltpu.SemaphoreType.DMA((n,)),
            pltpu.SemaphoreType.DMA((n, 2)),
        ]
        + (gather_scratch(sp) if extra else []),
        9 if extra else 10,
        qkv,
        *((h,) if extra else ()),
    )


def bwd_kernel(extra, *refs):
    if extra:
        (
            qkv_ref, kv_all, do_ref, mixt_ref, lse_ref, cos_ref, sin_ref, cos_n, sin_n,
            part_ref, h_ref, out_ref, y_ref,
            qt, dot, qn, don, dl_s, dqt, acc, got_r, got_l, put_r, put_l, sr, ar, sl, al,
            sc_got, sc_held, *sc,
        ) = refs
    else:
        (
            qkv_ref, kv_all, do_ref, mixt_ref, lse_ref, cos_ref, sin_ref, cos_n, sin_n, out_ref,
            qt, dot, qn, don, dl_s, dqt, acc, got_r, got_l, put_r, put_l, sr, ar, sl, al,
        ) = refs
    c, n, has_left, has_right = ctx_ends()
    n_t, _, sp, _ = qkv_ref.shape
    length, width = kv_all.shape[2:]
    kv_heads = width // (2 * HEAD_DIM)
    q_heads = qt.shape[1]
    q_w = q_heads * HEAD_DIM
    group = q_heads // kv_heads
    scale = HEAD_DIM**-0.5
    half = HEAD_DIM // 2

    def rightward(r):
        return along(put_r.at[r], got_r.at[r], sr.at[r], ar.at[r], c + 1)

    def leftward(r):
        return along(put_l.at[r], got_l.at[r], sl.at[r], al.at[r], c - 1)

    greet(tensor=extra, line=True)
    if extra:
        chunks = chunk_list(sp)
        for q in range(len(chunks)):
            scatter_start(part_ref, sc_got, sc, chunks, q)
    for j in range(2):
        x = qkv_ref[:, j, :, :q_w].reshape(length, q_w)
        y = do_ref[:, j].reshape(length, q_w)
        for h in range(q_heads):
            a = head_of(x, h)
            qn[j, h] = a
            qt[j, h] = transposed(a)
            b = head_of(y, h)
            don[j, h] = b
            bt = b.astype(F32).T
            dot[j, h] = bt.astype(BF)
            dl_s[j, h] = jnp.sum(bt * mixt_ref[j, h].astype(F32), axis=0, keepdims=True)
    dqt[...] = jnp.zeros_like(dqt)

    def pair(r, kj, j, masked):
        x = kv_all[r, kj]
        for kh in range(kv_heads):
            key = head_of(x, kh)
            value = head_of(x, kv_heads + kh)
            key_t = transposed(key)
            dk = acc[kj, kh]
            dv = acc[kj, kv_heads + kh]
            for g in range(group):
                h = kh * group + g
                s = nn(key, qt[j, h]) * (scale * LOG2E)
                p = jnp.exp2(s - lse_ref[j, h])
                if masked:
                    p = jnp.where(causal(length), p, 0.0)
                dp = nn(value, dot[j, h])
                ds = (p * (dp - dl_s[j, h])).astype(BF)
                dv = dv + nn(p.astype(BF), don[j, h])
                dk = dk + nn(ds, qn[j, h])
                dqt[j, h] += nn(key_t, ds)
            acc[kj, kh] = dk
            acc[kj, kv_heads + kh] = dv

    def joined(kj):
        parts = [acc[kj, i] * (scale if i < kv_heads else 1.0) for i in range(2 * kv_heads)]
        return jnp.concatenate(parts, axis=-1)

    def finish_right(r, has_more):
        @pl.when(has_more)
        def _():
            rightward(r).wait_recv()
            for kj in range(2):
                put_r[r, kj] = (put_r[r, kj].astype(F32) + got_r[r, kj].astype(F32)).astype(BF)

        rightward(r).start()

    def finish_left(r, has_more):
        @pl.when(has_more)
        def _():
            leftward(r).wait_recv()
            put_l[r] = (put_l[r].astype(F32) + got_l[r].astype(F32)).astype(BF)

        leftward(r).start()

    def step(i, _):
        s = n - 1 - i

        def one_side(side, _):
            r = jnp.where(side == 0, c + s, c - s)
            ready = jnp.where(side == 0, c + s < n, (c - s >= 0) & (s > 0))

            @pl.when(ready)
            def _():
                acc[...] = jnp.zeros_like(acc)

                @pl.when(s == 0)
                def _():
                    def diagonal(j, _):
                        pair(c, j, j, True)
                        return 0

                    lax.fori_loop(0, 2, diagonal, 0)

                def item(k, _):
                    @pl.when((s > 0) | (k == 0))
                    def _():
                        pair(r, jnp.where(side == 0, k, 0), jnp.where(side == 0, 1, k), False)

                    return 0

                lax.fori_loop(0, 2, item, 0)

                @pl.when((side == 0) & (s > 0))
                def _():
                    for kj in range(2):
                        put_r[r, kj] = joined(kj).astype(BF)

                    @pl.when(jnp.logical_not(has_left))
                    def _():
                        rightward(r).start()

                @pl.when(side == 1)
                def _():
                    put_l[r] = joined(0).astype(BF)

                    @pl.when(jnp.logical_not(has_right))
                    def _():
                        leftward(r).start()

            return 0

        lax.fori_loop(0, 2, one_side, 0)
        late = s + 1

        @pl.when((c + late < n) & has_left)
        def _():
            finish_right(c + late, has_left)

        @pl.when((c - late >= 0) & has_right)
        def _():
            finish_left(c - late, has_right)

        return 0

    lax.fori_loop(0, 2, step, 0)
    if extra:
        for q in range(len(chunks)):
            scatter_pass(part_ref, sc_got, sc_held, sc, chunks, q)
    lax.fori_loop(2, n, step, 0)
    if extra:
        for q in range(len(chunks)):
            j, at = chunks[q]
            term = scatter_end(part_ref, sc_got, sc_held, sc, chunks, q)
            y_ref[j, at] = (h_ref[j, at] + term).astype(BF)
        for q in range(len(chunks)):
            scatter_drain(part_ref, sc_got, sc, chunks, q)
    for j in range(2):
        outs = []
        for h in range(q_heads):
            d = dqt[j, h] * scale
            sc = d * sin_ref[j]
            back = d * cos_ref[j] + jnp.concatenate([sc[half:], -sc[:half]], axis=0)
            outs.append(back.T)
        out_ref[:, j, :, :q_w] = jnp.concatenate(outs, axis=-1).astype(BF).reshape(n_t, sp, q_w)

    @pl.when(has_right)
    def _():
        leftward(c).wait_recv()

    @pl.when(has_left)
    def _():
        rightward(c).wait_recv()

    for kj in range(2):
        total = joined(kj)
        total += jnp.where(has_left, got_r[c, kj].astype(F32), 0.0)
        if kj == 0:
            total += jnp.where(has_right, got_l[c].astype(F32), 0.0)
        parts = []
        for kh in range(2 * kv_heads):
            d = head_of(total, kh)
            if kh < kv_heads:
                sc = d * sin_n[kj]
                d = d * cos_n[kj] + jnp.concatenate([sc[:, half:], -sc[:, :half]], axis=1)
            parts.append(d)
        out_ref[:, kj, :, q_w:] = jnp.concatenate(parts, axis=-1).astype(BF).reshape(n_t, sp, width)

    def drain(r, _):
        @pl.when((r > c) & has_right)
        def _():
            rightward(r).wait_send()

        @pl.when((r < c) & has_left)
        def _():
            leftward(r).wait_send()

        return 0

    lax.fori_loop(0, n, drain, 0)


def flash_backward(qkv, kv_all, do, mixt, lse, tables, part=None, h=None):
    n, _, length, width = kv_all.shape
    q_heads = mixt.shape[1]
    cols = pltpu.VMEM((2, q_heads, HEAD_DIM, length), BF)
    natural = pltpu.VMEM((2, q_heads, length, HEAD_DIM), BF)
    both = pltpu.VMEM((n, 2, length, width), BF)
    early = pltpu.VMEM((n, length, width), BF)
    sems = pltpu.SemaphoreType.DMA((n,))
    extra = part is not None
    return call(
        functools.partial(bwd_kernel, extra),
        (jax.ShapeDtypeStruct(qkv.shape, BF),) + ((shapes_of(h)[3],) if extra else ()),
        [
            cols,
            cols,
            natural,
            natural,
            pltpu.VMEM((2, q_heads, 1, length), F32),
            pltpu.VMEM((2, q_heads, HEAD_DIM, length), F32),
            pltpu.VMEM((2, width // HEAD_DIM, length, HEAD_DIM), F32),
            both,
            early,
            both,
            early,
            sems,
            sems,
            sems,
            sems,
        ]
        + (scatter_scratch(h.shape[1], h.shape[2]) if extra else []),
        12 if extra else 11,
        qkv, kv_all, do, mixt, lse, *tables, *((part, h) if extra else ()),
    )


def feed_kernel(fwd, bwd, *refs):
    refs = list(refs)

    def take(size):
        out = refs[:size]
        del refs[:size]
        return out

    n2, w_gate, w_up, w_down = take(4)
    gm = take(1)[0] if bwd else None
    kept = take(2) if bwd and not fwd else None
    if fwd:
        y_ref = take(1)[0]
    if fwd and not bwd:
        keep = take(2)
    if bwd:
        part_ref, dw_gate, dw_up, dw_down = take(4)
    accs = refs
    step = pl.program_id(0)
    last = pl.num_programs(0) - 1

    def gather_up(out, acc, term):
        @pl.when(step == 0)
        def _():
            acc[...] = term

        @pl.when((step > 0) & (step < last))
        def _():
            acc[...] += term

        @pl.when(step == last)
        def _():
            out[...] = (acc[...] + term).astype(BF)

    if kept is None:
        x = n2[...]
        gate, up = nn(x, w_gate[...]), nn(x, w_up[...])
    else:
        gate, up = kept[0][...].astype(F32), kept[1][...].astype(F32)
    sig = jax.nn.sigmoid(gate)
    silu = gate * sig
    act = (silu * up).astype(BF)
    if fwd and not bwd:
        keep[0][...] = gate.astype(BF)
        keep[1][...] = up.astype(BF)
    if fwd:
        gather_up(y_ref, accs[0], nn(act, w_down[...]))
    if bwd:
        g = gm[...]
        dact = nt(g, w_down[...])
        dgate = (dact * up * (sig * (1.0 + gate * (1.0 - sig)))).astype(BF)
        dup = (dact * silu).astype(BF)
        gather_up(part_ref, accs[-1], nt(dgate, w_gate[...]) + nt(dup, w_up[...]))
        x = n2[...]
        dw_gate[...] = tn(x, dgate).astype(BF)
        dw_up[...] = tn(x, dup).astype(BF)
        dw_down[...] = tn(act, g).astype(BF)


def feed_call(layer, n2, w_gate, w_up, w_down, gm=None, kept=None):
    fwd, bwd = kept is None, gm is not None
    rows, d = n2.shape
    units = w_gate.shape[2]
    tile = min(512, units)
    once = pl.BlockSpec((rows, d), lambda i: (0, 0), pipeline_mode=pl.Buffered(1))
    out_once = pl.BlockSpec((rows, d), lambda i: (0, 0))
    weight = pl.BlockSpec((None, d, tile), lambda i: (layer, 0, i))
    weight_down = pl.BlockSpec((None, tile, d), lambda i: (layer, i, 0))
    col = pl.BlockSpec((d, tile), lambda i: (0, i))
    row = pl.BlockSpec((tile, d), lambda i: (i, 0))
    slab = pl.BlockSpec((rows, tile), lambda i: (0, i))
    operands, in_specs = [n2, w_gate, w_up, w_down], [once, weight, weight, weight_down]
    out, out_specs = [], []
    if bwd:
        operands.append(gm)
        in_specs.append(once)
    if bwd and not fwd:
        operands += kept
        in_specs += [slab, slab]
    full = jax.ShapeDtypeStruct((rows, d), BF)
    if fwd:
        out.append(full)
        out_specs.append(out_once)
    if fwd and not bwd:
        out += [jax.ShapeDtypeStruct((rows, units), BF)] * 2
        out_specs += [slab, slab]
    if bwd:
        out += [full] + [jax.ShapeDtypeStruct((d, units), BF)] * 2
        out.append(jax.ShapeDtypeStruct((units, d), BF))
        out_specs += [out_once, col, col, row]
    return pl.pallas_call(
        functools.partial(feed_kernel, fwd, bwd),
        grid=(units // tile,),
        in_specs=in_specs,
        out_specs=out_specs,
        out_shape=out,
        scratch_shapes=[pltpu.VMEM((rows, d), F32)] * (fwd + bwd),
        compiler_params=pltpu.CompilerParams(vmem_limit_bytes=60 * 2**20),
    )(*operands)


def settle_kernel(sec, mine0, mine1, got, *outs):
    def put(src):
        at = 0
        for out in outs:
            width = out.shape[1]
            out[...] = src[:, at : at + width].astype(F32)
            at += width

    other = pl.program_id(0) == 1

    @pl.when(other)
    def _():
        put(got)

    @pl.when(jnp.logical_not(other) & (sec[0] == 0))
    def _():
        put(mine0)

    @pl.when(jnp.logical_not(other) & (sec[0] == 1))
    def _():
        put(mine1)


def settle(sec, mine0, mine1, got, widths):
    rows, width = got.shape
    tile = 256 if rows % 256 == 0 else rows
    blocks = rows // tile
    block = (tile, width)
    return pl.pallas_call(
        settle_kernel,
        grid_spec=pltpu.PrefetchScalarGridSpec(
            num_scalar_prefetch=1,
            grid=(2, blocks),
            in_specs=[
                pl.BlockSpec(block, lambda p, i, sec: (i * (1 - p) * (1 - sec[0]), 0)),
                pl.BlockSpec(block, lambda p, i, sec: (i * (1 - p) * sec[0], 0)),
                pl.BlockSpec(block, lambda p, i, sec: (i * p, 0)),
            ],
            out_specs=[
                pl.BlockSpec((tile, w), lambda p, i, sec: (((p + sec[0]) % 2) * blocks + i, 0))
                for w in widths
            ],
        ),
        out_shape=[jax.ShapeDtypeStruct((2 * rows, w), F32) for w in widths],
        compiler_params=pltpu.CompilerParams(vmem_limit_bytes=32 * 2**20),
    )(sec, mine0, mine1, got)


def turn_matrix(heads, total):
    half = HEAD_DIM // 2
    m = np.zeros((total, total), np.float32)
    for h in range(heads):
        at = h * HEAD_DIM
        for i in range(half):
            m[at + half + i, at + i] = -1.0
            m[at + i, at + half + i] = 1.0
    return m


def swap(value):
    return lax.ppermute(value, "section", [(0, 1), (1, 0)])


def on_device(
    inputs, cotangent, block_order, attn_gain, w_query, key_weight, value_weight, w_out,
    mlp_gain, w_gate, w_up, w_down,
):
    sec = lax.axis_index("section")
    first = sec == 0
    ctx = lax.axis_index("ctx")
    n_t = lax.axis_size("tensor")
    n_ctx = lax.axis_size("ctx")
    _, _, _, sp, half_width = inputs.shape
    length = sp * n_t
    d = 2 * half_width
    rows = n_t * 2 * sp
    wq, wk, wv = w_query[0], key_weight[0], value_weight[0]
    q_w, kv_w = wq.shape[1], 2 * wk.shape[1]
    qkv_w = q_w + kv_w
    q_heads, kv_heads = q_w // HEAD_DIM, kv_w // (2 * HEAD_DIM)

    def to_own(x):
        keep = lax.dynamic_index_in_dim(x[:, 0], sec, 0, keepdims=False)
        give = lax.dynamic_index_in_dim(x[:, 0], 1 - sec, 0, keepdims=False)
        got = swap(give)
        return jnp.where(
            first, jnp.concatenate([keep, got], -1), jnp.concatenate([got, keep], -1)
        )

    def from_own(y, out_dtype):
        y = in_order(y)
        lo, hi = y[..., :half_width], y[..., half_width:]
        keep = jnp.where(first, lo, hi)
        got = swap(jnp.where(first, hi, lo).astype(BF)).astype(y.dtype)
        return jnp.where(first, jnp.stack([keep, got]), jnp.stack([got, keep]))[
            :, None
        ].astype(out_dtype)

    turned = lax.dynamic_index_in_dim(block_order, 2 * ctx, 0, keepdims=False) != ctx

    def in_order(x):
        return jnp.where(turned, jnp.stack([x[1], x[0]]), x)

    x_own = in_order(to_own(inputs))
    g_own = in_order(to_own(cotangent))

    turn_q = jnp.asarray(turn_matrix(q_heads, q_w), BF)
    turn_kv = turn_matrix(kv_heads, kv_w)
    wkv = jnp.concatenate([wk, wv], 1)
    wcat = jnp.concatenate(
        [wq, wkv, nn(wq, turn_q).astype(BF), nn(wkv, jnp.asarray(turn_kv, BF)).astype(BF)], 1
    )

    def both(w):
        return lax.all_gather(w, "section", axis=0)

    wcat2, wo2, wg2, wu2, wd2, gains2 = (
        both(wcat), both(w_out[0]), both(w_gate[0]), both(w_up[0]), both(w_down[0]),
        both(jnp.concatenate([attn_gain, mlp_gain], 0)),
    )

    def gain_of(layer, kind):
        return gains2[layer, kind : kind + 1]

    def tie(*values):
        return lax.optimization_barrier(values)

    flat = lambda v: v.reshape(rows, d)
    a0, a1, m0, m1 = gain_of(0, 0), gain_of(1, 0), gain_of(0, 1), gain_of(1, 1)

    h0 = x_own.astype(F32)
    n1_0 = flat(norm_gather(x_own, a0))

    own = jnp.stack([ctx, 2 * n_ctx - 1 - ctx])
    n1_0, own = tie(n1_0, own)
    offs = jnp.arange(length, dtype=jnp.int32)
    pos = own[:, None] * length + offs[None, :]
    freq = ROPE_BASE ** (-(jnp.arange(0, HEAD_DIM, 2).astype(F32) / HEAD_DIM))
    phase_t = freq[None, :, None] * pos.astype(F32)[:, None, :]
    phase_t = jnp.concatenate([phase_t, phase_t], 1)
    cos_t, sin_t = jnp.cos(phase_t), jnp.sin(phase_t)

    def rows_of(t):
        t = jnp.swapaxes(t, 1, 2).reshape(2, n_t, sp, HEAD_DIM)
        return jnp.swapaxes(t, 0, 1).reshape(rows, HEAD_DIM)

    cos_r, sin_r = rows_of(cos_t), rows_of(sin_t)
    cos_n, sin_n = jnp.swapaxes(cos_t, 1, 2), jnp.swapaxes(sin_t, 1, 2)
    spread = np.zeros((HEAD_DIM, qkv_w), np.float32)
    turned_w = q_w + kv_w // 2
    spread[np.arange(turned_w) % HEAD_DIM, np.arange(turned_w)] = 1.0
    plain = np.where(np.arange(qkv_w) < turned_w, 0.0, 1.0).astype(np.float32)

    def wide_table(t):
        return lax.dot_general(
            t,
            jnp.asarray(spread),
            (((1,), (0,)), ((), ())),
            precision=lax.Precision.HIGH,
            preferred_element_type=F32,
        )

    cos_all, sin_all = wide_table(cos_r) + jnp.asarray(plain), wide_table(sin_r)

    def attend(n1, layer, h=None):
        raw = nn(n1, wcat2[layer])
        qkv = (raw[:, :qkv_w] * cos_all + raw[:, qkv_w:] * sin_all).astype(BF)
        qkv = qkv.reshape(n_t, 2, sp, qkv_w)
        mix, mixt, lse, kv_all, *full = flash_forward(qkv, q_heads, h)
        mix = mix.reshape(rows, q_w)
        part = nn(mix, wo2[layer]).astype(BF)
        return part.reshape(n_t, 2, sp, d), (qkv, kv_all, mix, mixt, lse, *full)

    def in_blocks(part):
        return part.reshape(n_t, 2, sp, d)

    def attend_back(ga, layer, kept, *more):
        qkv, kv_all, _, mixt, lse = kept[:5]
        dmix = nt(ga, wo2[layer]).astype(BF).reshape(n_t, 2, sp, q_w)
        tables = (cos_t, sin_t, cos_n, sin_n)
        dqkv, *more = flash_backward(qkv, kv_all, dmix, mixt, lse, tables, *more)
        dqkv = dqkv.reshape(rows, qkv_w)
        part = nt(dqkv, wcat2[layer][:, :qkv_w]).astype(BF)
        return part.reshape(n_t, 2, sp, d), dqkv, more

    def halve(*grads):
        return [lax.psum_scatter(g, "section", scatter_dimension=0, tiled=True) for g in grads]

    def grad(left, right):
        return tn(left, right).astype(BF)

    def cut(size, term):
        return term.reshape(2, -1, size, term.shape[1])

    part, att0 = attend(n1_0, 0)
    h2_0, full = sum_norm_gather(part, h0, m0, 0)
    n2_0 = flat(full)
    part, *kept0 = feed_call(0, n2_0, wg2, wu2, wd2)
    part = in_blocks(part)
    h1, full = sum_norm_gather(part, h2_0, a1, 1)
    n1_1 = flat(full)
    part, att1 = attend(n1_1, 1, g_own)
    h2_1, full = sum_norm_gather(part, h1, m1, 2)
    n2_1 = flat(full)

    gm1 = flat(att1[5])
    def joined(zs):
        return [z.reshape(-1, z.shape[-1]) for z in zs]

    y_part, part, *raw = feed_call(1, n2_1, wg2, wu2, wd2, gm1)
    y_part, part = in_blocks(y_part), in_blocks(part)
    wide1, down1 = halve(*raw[:2]), halve(raw[2])
    dh2_1, dm1, _, (full,) = back(part, h2_1, m1, g_own.astype(F32), 0, 5, ())
    ga = flat(full)
    part, dqkv, (y,) = attend_back(ga, 1, att1, y_part, h2_1)
    raw = (grad(att1[2], ga), grad(n1_1, dqkv))
    part, raw, wide1 = tie(part, raw, wide1)
    rest1 = down1 + halve(*raw)
    zs = [cut(48, v) for v in wide1]
    g0, da1, wide1, (full,) = back(part, h1, a1, dh2_1, 1, 6, zs)
    gm0 = flat(full)
    part, *raw = feed_call(0, n2_0, wg2, wu2, wd2, gm0, kept0)
    part = in_blocks(part)
    part, raw, rest1 = tie(part, raw, rest1)
    wide0 = halve(*raw)
    zs = [cut(size, v) for size, v in zip((32, 32, 64), rest1)]
    dh2_0, dm0, rest1, (full,) = back(part, h2_0, m0, g0.astype(F32), 0, 7, zs)
    ga = flat(full)
    part, dqkv, _ = attend_back(ga, 0, att0)
    raw = (grad(att0[2], ga), grad(n1_0, dqkv))
    part, raw, wide0 = tie(part, raw, wide0)
    rest0 = halve(*raw)
    zs = [cut(size, v) for size, v in zip((48, 48, 32), wide0)]
    others = jnp.concatenate([dm0, da1, dm1], 0)
    dh0, gains, wide0, _ = back(part, h0, a0, dh2_0, 2, 8, zs, others)
    rest0, dh0, gains = tie(rest0, dh0, gains)
    rest0 = chain_sum([cut(size, v) for size, v in zip((32, 64), rest0)])
    wide1, rest1, wide0, rest0 = joined(wide1), joined(rest1), joined(wide0), joined(rest0)
    y, dh0, gains, wide1, rest1, wide0, rest0 = tie(y, dh0, gains, wide1, rest1, wide0, rest0)
    grads1 = (rest1[0], *wide1, *rest1[1:])
    grads0 = (wide0[2], *wide0[:2], *rest0)
    gains = gains + swap(gains)
    gain_own = lax.dynamic_slice_in_dim(gains, 2 * sec, 2, 0)

    def to_owner(r0, r1):
        got = swap(jnp.where(first, r1, r0))
        keep = jnp.where(first, r0, r1)
        return jnp.where(
            first, jnp.concatenate([keep, got], 0), jnp.concatenate([got, keep], 0)
        ).astype(F32)

    gd, gg, gu, go = (to_owner(a, b) for a, b in zip(grads0[:4], grads1[:4]))
    mine0, mine1 = grads0[4], grads1[4]
    got = swap(jnp.where(first, mine1, mine0))
    gq, gk, gv = settle(sec.reshape(1), mine0, mine1, got, (q_w, kv_w // 2, kv_w // 2))
    return (
        from_own(y, BF),
        from_own(dh0, F32),
        gain_own[0:1],
        gq[None],
        gk[None],
        gv[None],
        go[None],
        gain_own[1:2],
        gg[None],
        gu[None],
        gd[None],
    )


def solution(mesh):
    rows = P(None, "ctx", None, "tensor", "section")
    gain = P("section", None)
    col = P("section", None, "tensor")
    row = P("section", "tensor", None)
    return jax.shard_map(
        on_device,
        mesh=mesh,
        in_specs=(rows, rows, P(), gain, col, col, col, row, gain, col, col, row),
        out_specs=(rows, rows, gain, col, col, col, row, gain, col, col, row),
        check_vma=False,
    )
```
